128 devices in a mesh: tm: 8 (over y, core), space: 16 (over z, x).
Axes of the slice: x: 4, y: 4, z: 4, core: 2. Of those that a mesh axis runs over, the one named last changes fastest.
Arguments:
- dinv: bfloat16 [8, 1024, 1024], P('tm', 'space')
- coupling: bfloat16 [8, 1024, 1024], P('tm'), may hold values from -0.15625 to 0.15625
- owner_position: int32 [1024], P('space'), may hold values from 0 to 1023, as said below
- pattern: int32 [16, 4], P('space'), may hold values from 0 to 7, all different within a row
- basis: bfloat16 [1024, 512], replicated, may hold values from -0.25 to 0.25
Outputs:
- sigma: bfloat16 [8, 1024, 1024], P('tm', 'space')
- gradient: bfloat16 [8, 1024, 512], P('tm', 'space')
The draws below stay inside these ranges and needn't reach their ends.
Inputs may be any that keep to these rules, and one draw needn't show every extreme that they name: `owner_position`: A permutation; the rows of space device j (rows j*64 to (j+1)*64 - 1) take exactly 4 positions in each aligned block of 64 positions, namely positions o*64 + j*4 to o*64 + (j+1)*4 - 1. `pattern`: each row names 4 different blocks.
All inputs are finite; a program needn't handle non-finite values.
Results may differ from the reference program's by a relative error of at most 0.022.
Values may be sent and summed in bfloat16 or wider, within the bound.
A program may use at most 64 MiB of HBM per device.

```python
import jax
import jax.numpy as jnp
from jax import lax

B = 1024
H = 512
STEPS = 8
ROWS_DEV = 64
PAIR = 4
NB = 4
N_SPACE = 16


def draw_dinv(key, part):
    key = jax.random.fold_in(key, 1)
    first_key, second_key = jax.random.split(key)
    noise = jax.random.normal(first_key, (STEPS, B, B), jnp.float32)
    symmetric = (noise + jnp.swapaxes(noise, 1, 2)) * (0.5 / jnp.sqrt(B * 1.0))
    diagonal = jax.random.uniform(second_key, (STEPS, B), jnp.float32, 1.0, 3.0)
    eye_block = jnp.eye(B, dtype=jnp.float32)
    return (symmetric + diagonal[:, :, None] * eye_block[None, :, :]).astype(jnp.bfloat16)


def draw_owner_position(key, part):
    key = jax.random.fold_in(key, 2)
    keys = jax.random.split(key, N_SPACE)
    shuffled = jax.vmap(lambda single: jax.random.permutation(single, ROWS_DEV))(keys).astype(jnp.int32)
    source_block = jnp.arange(N_SPACE, dtype=jnp.int32)[:, None]
    owner_block = shuffled // PAIR
    slot_index = shuffled % PAIR
    positions = owner_block * ROWS_DEV + source_block * PAIR + slot_index
    return positions.reshape(B).astype(jnp.int32)


def levels(key, extent, cuts, smallest, high):
    gain = 1.0
    for position, blocks in cuts:
        steps = jax.random.uniform(jax.random.fold_in(jax.random.fold_in(key, 6), position), (blocks,), jnp.float32, smallest / len(cuts), high / len(cuts))
        gain = gain * jnp.repeat(jnp.exp(steps), extent[position] // blocks).reshape((-1,) + (1,) * (len(extent) - 1 - position))
    return gain


def choose_distinct(own_key, rows, number_of, top, lift):
    order = jax.random.permutation(jax.random.fold_in(own_key, 1), number_of)
    pull = order
    for power in range(3):
        pull = pull * pull // number_of
    pull = pull * lift // number_of
    tickets = jax.random.randint(jax.random.fold_in(own_key, 2), (rows, number_of), 0, 4096) + pull
    fixed_rows = jax.random.permutation(jax.random.fold_in(own_key, 3), rows)[jnp.arange(number_of) % rows]
    tickets = jnp.where(jnp.arange(rows)[:, None] == fixed_rows[None, :], 1 << 14, tickets)
    merit = tickets * number_of + jnp.arange(number_of)
    return lax.top_k(merit.astype(jnp.int32), top)[1].astype(jnp.int32)


def scatter_about(key, dims, deviation, limit, pieces=(), held_as=jnp.bfloat16):
    entries = deviation * jax.random.normal(key, dims, jnp.float32)
    if pieces:
        entries = entries * levels(key, dims, pieces, -0.22, 0.18)
    return jnp.clip(entries, -limit, limit).astype(held_as)


def setup_inputs(seed: int = 0) -> dict:
    key_list = jax.random.split(jax.random.key(seed), 6)
    dinv = draw_dinv(jax.random.fold_in(key_list[5], 71), 0)
    coupling = scatter_about(key_list[1], (STEPS, B, B), (5 * B // 4) ** -0.5, 0.15625, ((0, 8),))
    owner_position = draw_owner_position(jax.random.fold_in(key_list[5], 71), 0)
    pattern = choose_distinct(key_list[3], N_SPACE, B // 128, NB, 0)
    basis = scatter_about(key_list[4], (B, H), (B // 2) ** -0.5, 0.25)
    return {"dinv": dinv, "coupling": coupling, "owner_position": owner_position, "pattern": pattern, "basis": basis}


def reference(dinv, coupling, owner_position, pattern, basis):
    next_sigma = jnp.zeros((B, B), jnp.float32)
    blocks = []
    for step in range(STEPS - 1, -1, -1):
        carried = next_sigma.astype(jnp.bfloat16)
        product_rows = jnp.dot(coupling[step], carried, preferred_element_type=jnp.float32).astype(jnp.bfloat16)
        next_sigma = dinv[step].astype(jnp.float32) + jnp.dot(product_rows, coupling[step].T, preferred_element_type=jnp.float32)
        blocks.append(next_sigma.astype(jnp.bfloat16))
    sigma = jnp.stack(blocks[::-1])
    permuted = jnp.zeros_like(sigma).at[:, owner_position, :].set(sigma)
    column_block = jnp.arange(B, dtype=jnp.int32) // 128
    selected = jnp.any(pattern[:, :, None] == column_block[None, None, :], axis=1)
    masked = permuted.reshape(STEPS, N_SPACE, ROWS_DEV, B) * selected[None, :, None, :].astype(jnp.bfloat16)
    gradient = jnp.dot(masked.reshape(STEPS * B, B), basis, preferred_element_type=jnp.float32)
    return sigma, gradient.reshape(STEPS, B, H).astype(jnp.bfloat16)
```

```python
import jax
import jax.numpy as jnp
from jax import lax
from jax.experimental import pallas as pl
from jax.experimental.pallas import tpu as pltpu
from jax.sharding import PartitionSpec as P

MESH = pl.DeviceIdType.MESH
N = 1024
R = 64
SP = 16
F32 = jnp.float32
BF = jnp.bfloat16


def dot_nt(a, b):
    return lax.dot_general(a, b, (((1,), (1,)), ((), ())), preferred_element_type=F32)


def kernel(
    dinv_ref, coupling_ref, pos_ref, pattern_ref, basis_ref,
    sigma_ref, grad_ref,
    w, x2, zbuf, dbuf, eterm, vterm, state, arrived, sent_final, got_final,
    basis, pieces_out, pieces_in, rows_out, rows_in,
    local_sem, core_send, core_recv, shift_send, shift_recv, ex_send, ex_recv, rows_send, rows_recv, swap_send, swap_recv,
):
    tm, sp = lax.axis_index("tm"), lax.axis_index("space")
    y, c = tm // 2, tm % 2
    zc, xc = sp // 4, sp % 4
    other = 1 - c
    partner = (y * 2 + other, sp)
    chain_core = jnp.where((y == 1) | (y == 2), 1, 0)
    chain = c == chain_core
    y_odd = y % 2 == 1
    last = y == 3

    load_c = pltpu.make_async_copy(coupling_ref, w.at[c], local_sem.at[0])
    load_c.start()
    load_b = pltpu.make_async_copy(basis_ref, basis, local_sem.at[1])
    load_b.start()
    dbuf[pl.ds(c, 1)] = dinv_ref[...][None]

    barrier = pltpu.get_barrier_semaphore()

    def greet(t, s):
        pl.semaphore_signal(barrier, inc=1, device_id=(t, s), device_id_type=MESH)

    for d in range(1, SP):
        greet(tm, (sp + d) % SP)
    greet(*partner)
    for dy in (1, 3):
        for core in (0, 1):
            greet(((y + dy) % 4) * 2 + core, sp)
    pl.semaphore_wait(barrier, SP + 4)

    core_d = pltpu.make_async_remote_copy(
        src_ref=dinv_ref, dst_ref=dbuf.at[c], send_sem=core_send.at[0], recv_sem=core_recv.at[0],
        device_id=partner, device_id_type=MESH)
    core_d.start()
    load_c.wait()
    core_c = pltpu.make_async_remote_copy(
        src_ref=w.at[c], dst_ref=w.at[c], send_sem=core_send.at[1], recv_sem=core_recv.at[1],
        device_id=partner, device_id_type=MESH)
    core_c.start()

    lane = lax.broadcasted_iota(jnp.int32, (1, 1, 128), 2)
    low = lane < R
    pick = low != (sp % 2 == 1)
    eye = (lax.broadcasted_iota(jnp.int32, (256, 256), 0)
           == lax.broadcasted_iota(jnp.int32, (256, 256), 1)).astype(BF)

    def set_x(value):
        x2[0:R] = value
        x2[R:2 * R] = value

    def exchange(k, chunk):
        for dz in (2, 1, 3, 0):
            q = (zc + dz) % 4
            v = chunk(q).reshape(4, 2, 32, 128)
            packed = jnp.where(pick, v[:, 0], v[:, 1])
            pieces_out[k, pl.ds(4 * q, 4)] = packed.astype(BF)
            for dx in (2, 1, 3, 0):
                i = 4 * q + (xc + dx) % 4
                if dz == 0 and dx == 0:
                    pieces_in[k, pl.ds(sp, 1)] = pieces_out[k, pl.ds(sp, 1)]
                else:
                    pltpu.make_async_remote_copy(
                        src_ref=pieces_out.at[k, i], dst_ref=pieces_in.at[k, sp],
                        send_sem=ex_send.at[k], recv_sem=ex_recv.at[k],
                        device_id=(tm, i), device_id_type=MESH).start()

    def exchange_desc(k):
        return pltpu.make_async_remote_copy(
            src_ref=pieces_out.at[k, pl.ds(0, SP - 1)], dst_ref=pieces_in.at[k, pl.ds(0, SP - 1)],
            send_sem=ex_send.at[k], recv_sem=ex_recv.at[k], device_id=partner, device_id_type=MESH)

    def product_chunk(slot):
        def chunk(q):
            return dot_nt(w[slot, pl.ds(pl.multiple_of(256 * q, 256), 256), :], x2[...])
        return chunk

    def transpose_chunk(q):
        return dot_nt(eye, x2[:, pl.ds(pl.multiple_of(256 * q, 256), 256)])

    def collect(k):
        exchange_desc(k).wait_recv()
        lo = low[0]
        for m in range(8):
            a = pieces_in[k, 2 * m].astype(F32)
            b = pieces_in[k, 2 * m + 1].astype(F32)
            zbuf[0:32, 128 * m:128 * (m + 1)] = jnp.where(lo, a, b).astype(BF)
            zbuf[32:64, 128 * m:128 * (m + 1)] = pltpu.roll(jnp.where(lo, b, a), R, 1).astype(BF)

    @pl.when(chain & y_odd)
    def _():
        core_d.wait_recv()
        set_x(dbuf[0])
        exchange(0, transpose_chunk)
        set_x(dbuf[1])

        @pl.when(c == 1)
        def _():
            core_c.wait_recv()
        exchange(1, product_chunk(0))
        collect(0)
        vterm[...] = zbuf[...].astype(F32)

    @pl.when(chain & jnp.logical_not(y_odd))
    def _():
        core_d.wait_recv()
        set_x(dbuf[1])
        exchange(0, transpose_chunk)
        vterm[...] = dbuf[0].astype(F32)
        collect(0)
        set_x(zbuf[...])

        @pl.when(c == 1)
        def _():
            core_c.wait_recv()
        exchange(1, product_chunk(0))

    @pl.when(jnp.logical_not(chain))
    def _():
        core_d.wait_recv()
        eterm[...] = dbuf[1].astype(F32)

        @pl.when(c == 1)
        def _():
            core_c.wait_recv()

        @pl.when(y == 1)
        def _():
            set_x(dbuf[1])
            exchange(0, transpose_chunk)
            collect(0)
            eterm[...] = zbuf[...].astype(F32)

    @pl.when(c == 0)
    def _():
        @pl.when(jnp.logical_not(last))
        def _():
            core_c.wait_recv()

    @pl.when(chain & jnp.logical_not(last))
    def _():
        for part in range(4):
            w[2, 256 * part:256 * (part + 1), :] = jnp.dot(
                w[0, 256 * part:256 * (part + 1), :], w[1], preferred_element_type=F32).astype(BF)

    @pl.when(chain)
    def _():
        collect(1)
        eterm[...] = vterm[...] + dot_nt(zbuf[...], w[0])

    @pl.when(last)
    def _():
        state[...] = eterm[...].astype(BF)

        @pl.when(c == 0)
        def _():
            core_c.wait_recv()

    def shift_desc(core, k):
        return pltpu.make_async_remote_copy(
            src_ref=state, dst_ref=arrived, send_sem=shift_send.at[k], recv_sem=shift_recv,
            device_id=(((y + 3) % 4) * 2 + core, sp), device_id_type=MESH)

    @pl.when(jnp.logical_not(last))
    def _():
        slot = jnp.where(chain, 2, 1)
        shift_desc(c, 0).wait_recv()
        set_x(arrived[...])
        exchange(2, product_chunk(slot))
        collect(2)
        state[...] = (eterm[...] + dot_nt(zbuf[...], w[slot])).astype(BF)

    @pl.when(chain & (y > 0))
    def _():
        next_core = jnp.where(y == 1, 0, 1)
        shift_desc(next_core, 0).start()
        shift_desc(1 - next_core, 1).start()

    convert = y_odd & jnp.logical_not(last & jnp.logical_not(chain))

    @pl.when(convert)
    def _():
        set_x(state[...])
        exchange(3, transpose_chunk)
        collect(3)
        sent_final[...] = zbuf[...]

    @pl.when(jnp.logical_not(convert))
    def _():
        sent_final[...] = state[...]

    swap = pltpu.make_async_remote_copy(
        src_ref=sent_final, dst_ref=got_final, send_sem=swap_send, recv_sem=swap_recv,
        device_id=partner, device_id_type=MESH)

    @pl.when(chain_core == 1)
    def _():
        swap.start()
        swap.wait()

    @pl.when(chain_core == 0)
    def _():
        got_final[...] = sent_final[...]

    sigma_ref[...] = got_final[...]

    position = pos_ref[...]
    target = position // R * 4 + position % 4
    slots = lax.broadcasted_iota(jnp.int32, (R, R), 0)
    place = (slots == target).astype(BF)
    ordered = jnp.dot(place, got_final[...], preferred_element_type=F32).astype(BF)
    stacked = jnp.concatenate([ordered[:, 256 * k:256 * (k + 1)] for k in range(4)], axis=0)
    ri = lax.broadcasted_iota(jnp.int32, (256, 256), 0)
    ci = lax.broadcasted_iota(jnp.int32, (256, 256), 1)
    spread = (ci == (ri % 16) // 4 * R + ri // 16 * 4 + ri % 4).astype(BF)
    rows_out[...] = jnp.dot(spread, stacked, preferred_element_type=F32).astype(BF).reshape(SP, 16, 256)
    for d in (10, 6, 14, 2, 9, 11, 5, 7, 13, 15, 1, 3, 8, 4, 12):
        i = (sp + d) % SP
        pltpu.make_async_remote_copy(
            src_ref=rows_out.at[i], dst_ref=rows_in.at[sp], send_sem=rows_send, recv_sem=rows_recv,
            device_id=(tm, i), device_id_type=MESH).start()
    rows_in[pl.ds(sp, 1)] = rows_out[pl.ds(sp, 1)]
    load_b.wait()
    rows_desc = pltpu.make_async_remote_copy(
        src_ref=rows_out.at[pl.ds(0, SP - 1)], dst_ref=rows_in.at[pl.ds(0, SP - 1)],
        send_sem=rows_send, recv_sem=rows_recv, device_id=partner, device_id_type=MESH)
    rows_desc.wait_recv()
    gather = (ci == (ri % R) // 4 * 16 + ri // R * 4 + ri % 4).astype(BF)
    mine = jnp.dot(gather, rows_in[...].reshape(256, 256), preferred_element_type=F32).astype(BF)
    block = lax.broadcasted_iota(jnp.int32, (1, 256), 1) // 128
    total = jnp.zeros((R, grad_ref.shape[1]), F32)
    for k in range(4):
        chosen = jnp.zeros((1, 256), jnp.int32)
        for n in range(pattern_ref.shape[1]):
            chosen = jnp.where(block + 2 * k == pattern_ref[0, n], 1, chosen)
        masked = jnp.where(chosen == 1, mine[R * k:R * (k + 1)].astype(F32), 0.0).astype(BF)
        total += jnp.dot(masked, basis[256 * k:256 * (k + 1), :], preferred_element_type=F32)
    grad_ref[...] = total.astype(BF)

    core_d.wait_send()
    core_c.wait_send()
    rows_desc.wait_send()

    @pl.when(chain & (y > 0))
    def _():
        shift_desc(0, 0).wait_send()
        shift_desc(0, 1).wait_send()

    @pl.when(chain | (y == 1))
    def _():
        exchange_desc(0).wait_send()

    @pl.when(chain)
    def _():
        exchange_desc(1).wait_send()

    @pl.when(jnp.logical_not(last))
    def _():
        exchange_desc(2).wait_send()

    @pl.when(convert)
    def _():
        exchange_desc(3).wait_send()


def on_device(dinv, coupling, owner_position, pattern, basis):
    vmem = pl.BlockSpec(memory_space=pltpu.VMEM)
    anywhere = pl.BlockSpec(memory_space=pl.ANY)
    smem = pl.BlockSpec(memory_space=pltpu.SMEM)
    h = basis.shape[1]
    dma = pltpu.SemaphoreType.DMA
    sigma, gradient = pl.pallas_call(
        kernel,
        out_shape=(jax.ShapeDtypeStruct((R, N), BF), jax.ShapeDtypeStruct((R, h), BF)),
        in_specs=[vmem, anywhere, vmem, smem, anywhere],
        out_specs=(vmem, vmem),
        scratch_shapes=[
            pltpu.VMEM((3, N, N), BF),
            pltpu.VMEM((2 * R, N), BF),
            pltpu.VMEM((R, N), BF),
            pltpu.VMEM((2, R, N), BF),
            pltpu.VMEM((R, N), F32),
            pltpu.VMEM((R, N), F32),
            pltpu.VMEM((R, N), BF),
            pltpu.VMEM((R, N), BF),
            pltpu.VMEM((R, N), BF),
            pltpu.VMEM((R, N), BF),
            pltpu.VMEM((N, h), BF),
            pltpu.VMEM((4, SP, 32, 128), BF),
            pltpu.VMEM((4, SP, 32, 128), BF),
            pltpu.VMEM((SP, 16, 256), BF),
            pltpu.VMEM((SP, 16, 256), BF),
            dma((2,)), dma((2,)), dma((2,)), dma((2,)), dma, dma((4,)), dma((4,)), dma, dma, dma, dma,
        ],
        compiler_params=pltpu.CompilerParams(
            collective_id=0, has_side_effects=True, vmem_limit_bytes=48 << 20),
        name="selected_inverse",
    )(dinv[0], coupling[0], owner_position[None], pattern, basis)
    return sigma[None], gradient[None]


def solution(mesh):
    placed = (P("tm", "space", None), P("tm", None, None), P("space"), P("space", None), P())
    return jax.shard_map(
        on_device,
        mesh=mesh,
        in_specs=placed,
        out_specs=(P("tm", "space", None), P("tm", "space", None)),
        check_vma=False,
    )
```

```python
import jax
import jax.numpy as jnp
from jax import lax
from jax.experimental import pallas as pl
from jax.experimental.pallas import tpu as pltpu
from jax.sharding import PartitionSpec as P

MESH = pl.DeviceIdType.MESH
N = 1024
R = 64
SP = 16
F32 = jnp.float32
BF = jnp.bfloat16
FAR_FIRST = (10, 6, 14, 2, 9, 11, 5, 7, 13, 15, 1, 3, 8, 4, 12)


def dot_nt(a, b):
    return lax.dot_general(a, b, (((1,), (1,)), ((), ())), preferred_element_type=F32)


def dot_nn(a, b):
    return jnp.dot(a, b, preferred_element_type=F32)


def kernel(
    dinv_ref, coupling_ref, pos_ref, pattern_ref, basis_ref,
    sigma_ref, grad_ref,
    w, wt, wp, perm, x2, zbuf, dbuf, eterm, vterm, state, arrived, sent_final, final, basis,
    pos, pos_out, pos_in, pattern, pieces_out, pieces_in, rows_out, rows_in,
    local_sem, core_send, core_recv, shift_send, shift_recv, ex_send, ex_recv,
    rows_send, rows_recv, swap_send, swap_recv, pos_send, pos_recv,
):
    tm, sp = lax.axis_index("tm"), lax.axis_index("space")
    y, c = tm // 2, tm % 2
    zc, xc = sp // 4, sp % 4
    partner = (y * 2 + 1 - c, sp)
    chain_core = jnp.where((y == 1) | (y == 2), 1, 0)
    chain = c == chain_core
    y_odd = y % 2 == 1
    first_plane, last_plane = y == 0, y == 3
    idle = last_plane & jnp.logical_not(chain)
    no = jnp.logical_not

    load_d = pltpu.make_async_copy(dinv_ref, dbuf.at[c], local_sem.at[0])
    load_d.start()
    load_c = pltpu.make_async_copy(coupling_ref, w.at[c], local_sem.at[1])
    load_c.start()
    load_p = pltpu.make_async_copy(pos_ref, pos, local_sem.at[2])
    load_p.start()
    load_t = pltpu.make_async_copy(pattern_ref, pattern, local_sem.at[3])
    load_t.start()
    load_b = pltpu.make_async_copy(basis_ref, basis, local_sem.at[4])
    load_b.start()

    barrier = pltpu.get_barrier_semaphore()

    def greet(t, s):
        pl.semaphore_signal(barrier, inc=1, device_id=(t, s), device_id_type=MESH)

    for d in FAR_FIRST:
        greet(tm, (sp + d) % SP)
    for dy in (1, 3):
        for core in (0, 1):
            greet(((y + dy) % 4) * 2 + core, sp)
    greet(*partner)
    load_d.wait()
    load_p.wait()
    load_t.wait()
    load_c.wait()
    pl.semaphore_wait(barrier, SP + 4)

    core_d = pltpu.make_async_remote_copy(
        src_ref=dbuf.at[c], dst_ref=dbuf.at[c], send_sem=core_send.at[0], recv_sem=core_recv.at[0],
        device_id=partner, device_id_type=MESH)
    core_d.start()
    core_c = pltpu.make_async_remote_copy(
        src_ref=w.at[c], dst_ref=w.at[c], send_sem=core_send.at[1], recv_sem=core_recv.at[1],
        device_id=partner, device_id_type=MESH)
    core_c.start()

    lane = lax.broadcasted_iota(jnp.int32, (1, 1, 128), 2)
    low = lane < R
    pick = low != (sp % 2 == 1)
    ri = lax.broadcasted_iota(jnp.int32, (256, 256), 0)
    ci = lax.broadcasted_iota(jnp.int32, (256, 256), 1)
    eye = (ri == ci).astype(BF)

    def set_x(value):
        x2[0:R] = value
        x2[R:2 * R] = value

    def rows_of(ref, q):
        return ref[pl.ds(pl.multiple_of(256 * q, 256), 256), :]

    def exchange(k, *chunks):
        for dz in (2, 1, 3, 0):
            q = (zc + dz) % 4
            for h, chunk in enumerate(chunks):
                v = chunk(q).reshape(4, 2, 32, 128)
                packed = jnp.where(pick, v[:, 0], v[:, 1])
                pieces_out[k, pl.ds(4 * q, 4), h] = packed.astype(BF)
            for dx in (2, 1, 3, 0):
                i = 4 * q + (xc + dx) % 4
                if dz == 0 and dx == 0:
                    pieces_in[k, pl.ds(sp, 1)] = pieces_out[k, pl.ds(sp, 1)]
                else:
                    both = len(chunks) == 2
                    pltpu.make_async_remote_copy(
                        src_ref=pieces_out.at[k, i] if both else pieces_out.at[k, i, 0],
                        dst_ref=pieces_in.at[k, sp] if both else pieces_in.at[k, sp, 0],
                        send_sem=ex_send.at[k], recv_sem=ex_recv.at[k],
                        device_id=(tm, i), device_id_type=MESH).start()

    def exchange_desc(k, both):
        part = pl.ds(0, SP - 1)
        return pltpu.make_async_remote_copy(
            src_ref=pieces_out.at[k, part] if both else pieces_out.at[k, part, 0],
            dst_ref=pieces_in.at[k, part] if both else pieces_in.at[k, part, 0],
            send_sem=ex_send.at[k], recv_sem=ex_recv.at[k], device_id=partner, device_id_type=MESH)

    def product_chunk(slot):
        return lambda q: dot_nt(w[slot, pl.ds(pl.multiple_of(256 * q, 256), 256), :], x2[...])

    def transpose_chunk(q):
        return dot_nt(eye, x2[:, pl.ds(pl.multiple_of(256 * q, 256), 256)])

    def collect(k, both=False):
        exchange_desc(k, both).wait_recv()
        lo = low[0]
        for h in range(2 if both else 1):
            for m in range(8):
                a = pieces_in[k, 2 * m, h].astype(F32)
                b = pieces_in[k, 2 * m + 1, h].astype(F32)
                columns = slice(128 * m, 128 * (m + 1))
                zbuf[R * h:R * h + 32, columns] = jnp.where(lo, a, b).astype(BF)
                zbuf[R * h + 32:R * h + 64, columns] = pltpu.roll(jnp.where(lo, b, a), R, 1).astype(BF)

    def transpose_w(to, slot):
        for p in range(4):
            wt[to, :, 256 * p:256 * (p + 1)] = w[slot, 256 * p:256 * (p + 1), :].T

    def send_rows(value):
        position = pos[...]
        target = position // R * 4 + position % 4
        place = (lax.broadcasted_iota(jnp.int32, (R, R), 0) == target).astype(BF)
        ordered = dot_nn(place, value).astype(BF)
        stacked = jnp.concatenate([ordered[:, 256 * k:256 * (k + 1)] for k in range(4)], axis=0)
        spread = (ci == (ri % 16) // 4 * R + ri // 16 * 4 + ri % 4).astype(BF)
        rows_out[...] = dot_nn(spread, stacked).astype(BF).reshape(SP, 16, 256)
        for d in FAR_FIRST:
            i = (sp + d) % SP
            pltpu.make_async_remote_copy(
                src_ref=rows_out.at[i], dst_ref=rows_in.at[sp], send_sem=rows_send, recv_sem=rows_recv,
                device_id=(tm, i), device_id_type=MESH).start()
        rows_in[pl.ds(sp, 1)] = rows_out[pl.ds(sp, 1)]

    rows_desc = pltpu.make_async_remote_copy(
        src_ref=rows_out.at[pl.ds(0, SP - 1)], dst_ref=rows_in.at[pl.ds(0, SP - 1)],
        send_sem=rows_send, recv_sem=rows_recv, device_id=partner, device_id_type=MESH)

    def collect_rows():
        rows_desc.wait_recv()
        gather = (ci == (ri % R) // 4 * 16 + ri // R * 4 + ri % 4).astype(BF)
        return dot_nn(gather, rows_in[...].reshape(256, 256))

    @pl.when(chain & y_odd)
    def _():
        core_d.wait_recv()
        set_x(dbuf[1])

        @pl.when(c == 1)
        def _():
            core_c.wait_recv()
        exchange(1, product_chunk(0))
        set_x(dbuf[0])
        exchange(0, transpose_chunk)

    @pl.when(chain & no(y_odd))
    def _():
        core_d.wait_recv()
        set_x(dbuf[1])
        exchange(0, transpose_chunk)
        vterm[0:R] = dbuf[0].astype(F32)

    @pl.when(no(chain))
    def _():
        core_d.wait_recv()
        eterm[0:R] = dbuf[1].astype(F32)

        @pl.when(y == 1)
        def _():
            set_x(dbuf[1])
            exchange(0, transpose_chunk)

    permuted = first_plane | (y_odd & no(idle))

    def pos_desc(j, i):
        return pltpu.make_async_remote_copy(
            src_ref=pos_out, dst_ref=pos_in.at[j], send_sem=pos_send, recv_sem=pos_recv,
            device_id=(tm, i), device_id_type=MESH)

    @pl.when(permuted)
    def _():
        pos_out[...] = jnp.broadcast_to(jnp.concatenate([pos[...], pos[...]], axis=1), (8, 128))
        for d in FAR_FIRST:
            pos_desc(sp, (sp + d) % SP).start()
        pos_in[pl.ds(sp, 1)] = pos_out[...][None]

    @pl.when(first_plane | idle)
    def _():
        send_rows(dbuf[c])

    @pl.when(chain)
    def _():
        @pl.when(c == 1)
        def _():
            @pl.when(no(y_odd))
            def _():
                core_c.wait_recv()
        transpose_w(0, 0)

    pos_all = pltpu.make_async_remote_copy(
        src_ref=pos_in.at[pl.ds(0, SP - 1)], dst_ref=pos_in.at[pl.ds(0, SP - 1)],
        send_sem=pos_send, recv_sem=pos_recv, device_id=partner, device_id_type=MESH)

    @pl.when(permuted)
    def _():
        pos_all.wait_recv()
        p_index = lax.broadcasted_iota(jnp.int32, (N, 128), 0)
        for m in range(8):
            row = jnp.where(low[0], pos_in[2 * m, 0:1], pos_in[2 * m + 1, 0:1])
            perm[:, 128 * m:128 * (m + 1)] = (p_index == row).astype(BF)

    def permuted_chunk(ref):
        return lambda q: dot_nn(rows_of(perm, q), ref[...])

    @pl.when(chain & no(y_odd))
    def _():
        collect(0)
        set_x(zbuf[0:R])

        @pl.when(first_plane)
        def _():
            wp[:, 0:128] = dot_nt(w[0], x2[...]).astype(BF)
            exchange(1, lambda q: rows_of(wp, q)[:, 0:128].astype(F32), permuted_chunk(wp.at[:, 0:128]))

        @pl.when(no(first_plane))
        def _():
            exchange(1, product_chunk(0))

    @pl.when((y_odd & chain) | (no(chain) & (y == 1)))
    def _():
        collect(0)

        @pl.when(chain)
        def _():
            vterm[0:R] = zbuf[0:R].astype(F32)

        @pl.when(no(chain))
        def _():
            eterm[0:R] = zbuf[0:R].astype(F32)

    @pl.when(no(chain & (c == 1)))
    def _():
        core_c.wait_recv()

    @pl.when(chain & no(last_plane))
    def _():
        for part in range(4):
            rows = slice(256 * part, 256 * (part + 1))
            w[2, rows, :] = dot_nn(w[0, rows, :], w[1]).astype(BF)
        transpose_w(1, 2)

    @pl.when(no(chain) & no(last_plane))
    def _():
        transpose_w(1, 1)

    slot = jnp.where(chain, 2, 1)

    @pl.when(first_plane)
    def _():
        own = collect_rows()
        for k in range(4):
            columns = slice(256 * k, 256 * (k + 1))
            vterm[R:2 * R, columns] = own[R * k:R * (k + 1)]
        eterm[R:2 * R] = vterm[R:2 * R]

    @pl.when(chain)
    def _():
        @pl.when(first_plane)
        def _():
            collect(1, True)
            eterm[...] = vterm[...] + dot_nn(zbuf[...], wt[0])

        @pl.when(no(first_plane))
        def _():
            collect(1)
            eterm[0:R] = vterm[0:R] + dot_nn(zbuf[0:R], wt[0])

    @pl.when(first_plane)
    def _():
        for part in range(4):
            rows = slice(256 * part, 256 * (part + 1))
            wp[rows, :] = dot_nn(perm[rows, :], w[slot]).astype(BF)

    next_core = jnp.where(y == 1, 0, 1)

    def shift(n, core, k):
        return pltpu.make_async_remote_copy(
            src_ref=state.at[n], dst_ref=arrived.at[n], send_sem=shift_send.at[k], recv_sem=shift_recv,
            device_id=(((y + 3) % 4) * 2 + core, sp), device_id_type=MESH)

    def shift_all(k):
        return pltpu.make_async_remote_copy(
            src_ref=state, dst_ref=arrived, send_sem=shift_send.at[k], recv_sem=shift_recv,
            device_id=(((y + 3) % 4) * 2, sp), device_id_type=MESH)

    @pl.when(last_plane)
    def _():
        for n in range(4):
            state[n] = eterm[0:R, 256 * n:256 * (n + 1)].astype(BF)

            @pl.when(chain)
            def _():
                shift(n, next_core, 0).start()

    @pl.when(no(last_plane))
    def _():
        shift_all(0).wait_recv()
        for n in range(4):
            for h in range(2):
                x2[R * h:R * (h + 1), 256 * n:256 * (n + 1)] = arrived[n]

    @pl.when(no(last_plane) & no(first_plane))
    def _():
        exchange(2, product_chunk(slot))
        collect(2)
        for n in range(4):
            columns = slice(256 * n, 256 * (n + 1))
            state[n] = (eterm[0:R, columns] + dot_nn(zbuf[0:R], wt[1, :, columns])).astype(BF)

            @pl.when(chain)
            def _():
                shift(n, next_core, 0).start()

    @pl.when(chain & no(first_plane))
    def _():
        for n in range(4):
            shift(n, 1 - next_core, 1).start()

    @pl.when(first_plane)
    def _():
        exchange(2, product_chunk(slot), lambda q: dot_nt(rows_of(wp, q), x2[...]))
        collect(2, True)
        final[...] = (eterm[...] + dot_nn(zbuf[...], wt[1])).astype(BF)

    def swap(rows):
        return pltpu.make_async_remote_copy(
            src_ref=sent_final.at[pl.ds(0, rows)], dst_ref=final.at[pl.ds(0, rows)],
            send_sem=swap_send, recv_sem=swap_recv, device_id=partner, device_id_type=MESH)

    convert = y_odd & no(idle)

    @pl.when(convert)
    def _():
        for n in range(4):
            for h in range(2):
                x2[R * h:R * (h + 1), 256 * n:256 * (n + 1)] = state[n]
        exchange(3, transpose_chunk, lambda q: dot_nt(rows_of(perm, q), x2[...]))
        collect(3, True)

        @pl.when(y == 1)
        def _():
            sent_final[...] = zbuf[...]
            swap(2 * R).start()
            swap(2 * R).wait()

        @pl.when(last_plane)
        def _():
            final[...] = zbuf[...]

    @pl.when(y == 2)
    def _():
        for n in range(4):
            sent_final[0:R, 256 * n:256 * (n + 1)] = state[n]
        swap(R).start()
        swap(R).wait()
        send_rows(final[0:R])

    @pl.when(idle)
    def _():
        final[0:R] = dbuf[1]

    @pl.when(idle | (y == 2))
    def _():
        own = collect_rows().astype(BF)
        for k in range(4):
            final[R:2 * R, 256 * k:256 * (k + 1)] = own[R * k:R * (k + 1)]

    sigma_ref[...] = final[0:R]
    load_b.wait()
    block = lax.broadcasted_iota(jnp.int32, (1, N), 1) // 128
    chosen = jnp.zeros((1, N), jnp.int32)
    for n in range(pattern_ref.shape[1]):
        chosen = jnp.where(block == pattern[0, n], 1, chosen)
    masked = jnp.where(chosen == 1, final[R:2 * R].astype(F32), 0.0).astype(BF)
    grad_ref[...] = dot_nn(masked, basis[...]).astype(BF)

    core_d.wait_send()
    core_c.wait_send()

    @pl.when(first_plane | idle | (y == 2))
    def _():
        rows_desc.wait_send()

    @pl.when(permuted)
    def _():
        pos_all.wait_send()

    @pl.when(chain & no(first_plane))
    def _():
        shift_all(0).wait_send()
        shift_all(1).wait_send()

    @pl.when(chain | (y == 1))
    def _():
        exchange_desc(0, False).wait_send()

    @pl.when(chain & no(first_plane))
    def _():
        exchange_desc(1, False).wait_send()

    @pl.when(chain & first_plane)
    def _():
        exchange_desc(1, True).wait_send()

    @pl.when(first_plane)
    def _():
        exchange_desc(2, True).wait_send()

    @pl.when(no(last_plane) & no(first_plane))
    def _():
        exchange_desc(2, False).wait_send()

    @pl.when(convert)
    def _():
        exchange_desc(3, True).wait_send()


def on_device(dinv, coupling, owner_position, pattern, basis):
    vmem = pl.BlockSpec(memory_space=pltpu.VMEM)
    hbm = pl.BlockSpec(memory_space=pltpu.HBM)
    h = basis.shape[1]
    dma = pltpu.SemaphoreType.DMA
    sigma, gradient = pl.pallas_call(
        kernel,
        out_shape=(jax.ShapeDtypeStruct((R, N), BF), jax.ShapeDtypeStruct((R, h), BF)),
        in_specs=[hbm] * 5,
        out_specs=(vmem, vmem),
        scratch_shapes=[
            pltpu.VMEM((3, N, N), BF),
            pltpu.VMEM((2, N, N), BF),
            pltpu.VMEM((N, N), BF),
            pltpu.VMEM((N, N), BF),
            pltpu.VMEM((2 * R, N), BF),
            pltpu.VMEM((2 * R, N), BF),
            pltpu.VMEM((2, R, N), BF),
            pltpu.VMEM((2 * R, N), F32),
            pltpu.VMEM((2 * R, N), F32),
            pltpu.VMEM((4, R, 256), BF),
            pltpu.VMEM((4, R, 256), BF),
            pltpu.VMEM((2 * R, N), BF),
            pltpu.VMEM((2 * R, N), BF),
            pltpu.VMEM((N, h), BF),
            pltpu.VMEM((1, R), jnp.int32),
            pltpu.VMEM((8, 128), jnp.int32),
            pltpu.VMEM((SP, 8, 128), jnp.int32),
            pltpu.SMEM((1, 4), jnp.int32),
            pltpu.VMEM((4, SP, 2, 32, 128), BF),
            pltpu.VMEM((4, SP, 2, 32, 128), BF),
            pltpu.VMEM((SP, 16, 256), BF),
            pltpu.VMEM((SP, 16, 256), BF),
            dma((5,)), dma((2,)), dma((2,)), dma((2,)), dma, dma((4,)), dma((4,)), dma, dma, dma, dma, dma, dma,
        ],
        compiler_params=pltpu.CompilerParams(
            collective_id=0, has_side_effects=True, vmem_limit_bytes=48 << 20),
        name="selected_inverse",
    )(*[
        pltpu.with_memory_space_constraint(a, pltpu.HBM)
        for a in (dinv[0], coupling[0], owner_position[None], pattern, basis)
    ])
    return sigma[None], gradient[None]


def solution(mesh):
    placed = (P("tm", "space", None), P("tm", None, None), P("space"), P("space", None), P())
    return jax.shard_map(
        on_device,
        mesh=mesh,
        in_specs=placed,
        out_specs=(P("tm", "space", None), P("tm", "space", None)),
        check_vma=False,
    )
```

```python
import jax
import jax.numpy as jnp
from jax import lax
from jax.experimental import pallas as pl
from jax.experimental.pallas import tpu as pltpu
from jax.sharding import PartitionSpec as P

MESH = pl.DeviceIdType.MESH
N = 1024
R = 64
SP = 16
F32 = jnp.float32
BF = jnp.bfloat16
FAR_FIRST = (10, 6, 14, 2, 9, 11, 5, 7, 13, 15, 1, 3, 8, 4, 12)


def dot_nt(a, b):
    return lax.dot_general(a, b, (((1,), (1,)), ((), ())), preferred_element_type=F32)


def dot_nn(a, b):
    return jnp.dot(a, b, preferred_element_type=F32)


def kernel(
    dinv_ref, coupling_ref, pos_ref, pattern_ref, basis_ref,
    sigma_ref, grad_ref,
    w, wt, wp, perm, x2, x3, zbuf, dbuf, eterm, vterm, state, arrived, u_out, u_in, d_in, sent_final, final, basis,
    pos, pos_out, pos_in, pattern, pieces_out, pieces_in, rows_out, rows_in,
    local_sem, core_send, core_recv, shift_send, shift_recv, u_send, u_recv, d_recv, ex_send, ex_recv,
    rows_send, rows_recv, swap_send, swap_recv, pos_send, pos_recv, part_send, part_recv, share_send, share_recv,
):
    tm, sp = lax.axis_index("tm"), lax.axis_index("space")
    y, c = tm // 2, tm % 2
    zc, xc = sp // 4, sp % 4
    partner = (y * 2 + 1 - c, sp)
    is_a = c == jnp.where(y == 2, 1, 0)
    is_b = jnp.logical_not(is_a)
    quarter = (zc % 2) * 2 + xc % 2

    def when(condition, work):
        pl.when(condition)(work)

    def loop(count, work):
        def step(index, carry):
            work(index)
            return carry
        lax.fori_loop(0, count, step, 0)

    def block(index, size=256):
        return pl.ds(pl.multiple_of(size * index, size), size)

    def remote(src, dst, send, recv, device):
        return pltpu.make_async_remote_copy(
            src_ref=src, dst_ref=dst, send_sem=send, recv_sem=recv, device_id=device, device_id_type=MESH)

    load_d = pltpu.make_async_copy(dinv_ref, dbuf.at[c], local_sem.at[0])
    load_c = pltpu.make_async_copy(coupling_ref, w.at[c], local_sem.at[1])
    load_p = pltpu.make_async_copy(pos_ref, pos, local_sem.at[2])
    load_t = pltpu.make_async_copy(pattern_ref, pattern, local_sem.at[3])
    load_b = pltpu.make_async_copy(basis_ref, basis, local_sem.at[4])
    for load in (load_c, load_d, load_p, load_t, load_b):
        load.start()

    barrier = pltpu.get_barrier_semaphore()

    def greet(t, s):
        pl.semaphore_signal(barrier, inc=1, device_id=(t, s), device_id_type=MESH)

    for d in FAR_FIRST:
        greet(tm, (sp + d) % SP)
    for dy in (2, 1, 3):
        for core in (0, 1):
            greet(((y + dy) % 4) * 2 + core, sp)
    greet(*partner)

    lane = lax.broadcasted_iota(jnp.int32, (1, 1, 128), 2)
    low = lane < R
    lo = low[0]
    pick = low != (sp % 2 == 1)
    pick2 = pick[0]
    ri = lax.broadcasted_iota(jnp.int32, (256, 256), 0)
    ci = lax.broadcasted_iota(jnp.int32, (256, 256), 1)
    eye = (ri == ci).astype(BF)

    def transpose_w(to, slot):
        loop(4, lambda p: wt.__setitem__((to, slice(None), block(p)), w[slot, block(p), :].T))

    load_c.wait()
    when((c == 0) & (y != 2), lambda: transpose_w(0, 0))
    when((c == 1) & (y < 3), lambda: transpose_w(1, 1))
    load_d.wait()
    load_p.wait()
    load_t.wait()
    pl.semaphore_wait(barrier, SP + 6)

    core_d = remote(dbuf.at[c], dbuf.at[c], core_send.at[0], core_recv.at[0], partner)
    core_c = remote(w.at[c], w.at[c], core_send.at[1], core_recv.at[1], partner)
    copy_core = remote(w.at[3], w.at[3], core_send.at[2], core_recv.at[2], partner)
    gives_d = (c == 1) | (y == 2)
    gives_c = ((c == 1) & (y < 3)) | (y == 2)

    def part(slot, k):
        rows = pl.ds(pl.multiple_of(256 * quarter + 64 * k, 64), 64)
        return remote(w.at[slot, rows], w.at[3, rows], part_send, part_recv.at[k], (((y + 3) % 4) * 2 + 1, sp))

    def parts_sent(slot):
        return remote(w.at[slot, pl.ds(0, 256)], w.at[3, pl.ds(0, 256)], part_send, part_recv.at[0], partner)

    def share(k):
        part(3, k).wait_recv()
        first = 256 * quarter + 64 * k
        xs, zs = ((xc + 1) % 4, (xc + 3) % 4), ((zc + 1) % 4, (zc + 3) % 4)
        to = [(4 * zs[0] + xs[0], 0, 16), (4 * zs[0] + xs[1], 16, 16), (4 * zs[1] + xs[0], 32, 16), (4 * zs[1] + xs[1], 48, 16),
              (4 * zc + xs[0], 0, 32), (4 * zc + xs[1], 32, 32), (4 * zs[0] + xc, 0, 32), (4 * zs[1] + xc, 32, 32)]
        for device, offset, count in to:
            rows = pl.ds(pl.multiple_of(first + offset, 16), count)
            remote(w.at[3, rows], w.at[3, rows], share_send, share_recv, (tm, device)).start()

    shared = remote(w.at[3, pl.ds(0, 768)], w.at[3, pl.ds(0, 768)], share_send, share_recv, partner)

    def set_x(ref, value):
        ref[0:R] = value
        ref[R:2 * R] = value

    def set_x_blocks(blocks):
        for n in range(4):
            for h in range(2):
                x2[R * h:R * (h + 1), 256 * n:256 * (n + 1)] = blocks[n]

    def exchange(k, make):
        def row(step):
            dz = jnp.where(step == 0, 2, jnp.where(step == 1, 1, jnp.where(step == 2, 3, 0)))
            q = (zc + dz) % 4
            make(q, pieces_out.at[k, pl.ds(4 * q, 4)])
            for dx in (2, 1, 3, 0):
                i = 4 * q + (xc + dx) % 4

                def send(i=i):
                    remote(pieces_out.at[k, i], pieces_in.at[k, sp], ex_send.at[k], ex_recv.at[k], (tm, i)).start()
                if dx:
                    send()
                else:
                    when(dz != 0, send)
        loop(4, row)
        pieces_in[k, pl.ds(sp, 1)] = pieces_out[k, pl.ds(sp, 1)]

    def exchanged(k):
        some = pl.ds(0, SP - 1)
        return remote(pieces_out.at[k, some], pieces_in.at[k, some], ex_send.at[k], ex_recv.at[k], partner)

    def packed(*chunks):
        def make(q, out):
            for h, chunk in enumerate(chunks):
                v = chunk(q).reshape(4, 2, 32, 128)
                out[:, h] = jnp.where(pick, v[:, 0], v[:, 1]).astype(BF)
        return make

    def paired(chunk):
        def make(q, out):
            out[...] = chunk(q).reshape(4, 2, 32, 128).astype(BF)
        return make

    def collect(k, pair=False):
        exchanged(k).wait_recv()

        def columns(m):
            for h in range(2):
                a = pieces_in[k, 2 * m, h].astype(F32)
                b = pieces_in[k, 2 * m + 1, h].astype(F32)
                one, two = (32 * h, R + 32 * h) if pair else (R * h, R * h + 32)
                zbuf[one:one + 32, block(m, 128)] = jnp.where(lo, a, b).astype(BF)
                zbuf[two:two + 32, block(m, 128)] = pltpu.roll(jnp.where(lo, b, a), R, 1).astype(BF)
        loop(8, columns)

    def product_chunk(slot):
        return lambda q: dot_nt(w[slot, block(q), :], x2[...])

    def transpose_chunk(q):
        return dot_nt(eye, x2[:, block(q)])

    def perm_chunk(q):
        return dot_nt(perm[block(q), :], x2[...])

    def wp_chunk(q):
        return dot_nt(wp[block(q), :], x2[...])

    def level_chunk(q):
        return jnp.where(pick2, dot_nt(w[0, block(q), :], x2[...]), dot_nt(eye, x3[:, block(q)]))

    def send_positions():
        pos_out[...] = jnp.broadcast_to(jnp.concatenate([pos[...], pos[...]], axis=1), (8, 128))
        for d in FAR_FIRST:
            remote(pos_out, pos_in.at[sp], pos_send, pos_recv, (tm, (sp + d) % SP)).start()
        pos_in[pl.ds(sp, 1)] = pos_out[...][None]

    positions = remote(pos_in.at[pl.ds(0, SP - 1)], pos_in.at[pl.ds(0, SP - 1)], pos_send, pos_recv, partner)

    def make_perm():
        positions.wait_recv()
        p_index = lax.broadcasted_iota(jnp.int32, (N, 128), 0)

        def columns(m):
            row = jnp.where(lo, pos_in[2 * m, 0:1], pos_in[2 * m + 1, 0:1])
            perm[:, block(m, 128)] = (p_index == row).astype(BF)
        loop(8, columns)

    def make_wp(slot):
        loop(4, lambda p: wp.__setitem__((block(p), slice(None)), dot_nn(perm[block(p), :], w[slot]).astype(BF)))

    def send_rows(value):
        position = pos[...]
        target = position // R * 4 + position % 4
        place = (lax.broadcasted_iota(jnp.int32, (R, R), 0) == target).astype(BF)
        ordered = dot_nn(place, value).astype(BF)
        stacked = jnp.concatenate([ordered[:, 256 * k:256 * (k + 1)] for k in range(4)], axis=0)
        spread = (ci == (ri % 16) // 4 * R + ri // 16 * 4 + ri % 4).astype(BF)
        rows_out[...] = dot_nn(spread, stacked).astype(BF).reshape(SP, 16, 256)
        for d in FAR_FIRST:
            i = (sp + d) % SP
            remote(rows_out.at[i], rows_in.at[sp], rows_send, rows_recv, (tm, i)).start()
        rows_in[pl.ds(sp, 1)] = rows_out[pl.ds(sp, 1)]

    rows_sent = remote(rows_out.at[pl.ds(0, SP - 1)], rows_in.at[pl.ds(0, SP - 1)], rows_send, rows_recv, partner)

    def collect_rows(ref):
        rows_sent.wait_recv()
        gather = (ci == (ri % R) // 4 * 16 + ri // R * 4 + ri % 4).astype(BF)
        own = dot_nn(gather, rows_in[...].reshape(256, 256))
        for k in range(4):
            ref[R:2 * R, 256 * k:256 * (k + 1)] = own[R * k:R * (k + 1)].astype(ref.dtype)

    def shift(n, k, ref, recv, device):
        return remote(state.at[n], ref.at[n], shift_send.at[k], recv, (device, sp))

    def shifted(k):
        return remote(state, arrived, shift_send.at[k], shift_recv, partner)

    u_sent = remote(u_out, u_in, u_send.at[0], u_recv, (5, sp))
    d_sent = remote(dbuf.at[0], d_in, u_send.at[1], d_recv, (5, sp))

    give_v = remote(d_in, d_in, u_send.at[1], d_recv, partner)
    when(gives_d, core_d.start)
    when(gives_c, core_c.start)

    @pl.when(is_a)
    def _():
        @pl.when(y == 3)
        def _():
            d_sent.start()
            part(0, 0).start()
            part(0, 1).start()
        core_d.wait_recv()

        @pl.when(y == 3)
        def _():
            def columns(n):
                u_out[n] = dot_nn(dbuf[1], wt[0, :, block(n)]).astype(BF)
                remote(u_out.at[n], u_in.at[n], u_send.at[0], u_recv, (5, sp)).start()
            loop(4, columns)
            part(0, 2).start()
            part(0, 3).start()
        set_x(x2, dbuf[1])
        set_x(x3, dbuf[0])

        @pl.when(y == 2)
        def _():
            share(0)
            core_c.wait_recv()
        exchange(0, paired(level_chunk))

        @pl.when(y == 2)
        def _():
            share(1)
            d_sent.wait_recv()
            u_sent.wait_recv()
            odd = sp % 2
            for n in range(4):
                x2[pl.ds(pl.multiple_of(R * odd, R), R), 256 * n:256 * (n + 1)] = u_in[n]
            x2[pl.ds(pl.multiple_of(R * (1 - odd), R), R), :] = d_in[...]
            x3[...] = x2[...]
            loop(4, lambda n: x2.__setitem__((slice(None), block(n)), dot_nn(x3[...], wt[1, :, block(n)]).astype(BF)))
            exchange(1, paired(product_chunk(0)))
            share(2)
            share(3)
            transpose_w(0, 0)
        send_positions()

        @pl.when(y < 2)
        def _():
            core_c.wait_recv()
            w[2, block(quarter), :] = dot_nn(w[0, block(quarter), :], w[1]).astype(BF)

            @pl.when(y == 1)
            def _():
                for k in range(4):
                    part(2, k).start()
        collect(0, True)

        @pl.when(y != 2)
        def _():
            loop(4, lambda n: state.__setitem__(
                n, (dot_nn(zbuf[0:R], wt[0, :, block(n)]) + zbuf[R:2 * R, block(n)].astype(F32)).astype(BF)))

            @pl.when(y == 3)
            def _():
                for n in range(4):
                    shift(n, 0, arrived, shift_recv, 4).start()

            @pl.when(y == 1)
            def _():
                for core in (0, 1):
                    for n in range(4):
                        shift(n, core, u_in, u_recv, core).start()

        @pl.when(y == 2)
        def _():
            vterm[...] = zbuf[...].astype(F32)
            collect(1, True)
            shared.wait_recv()

            def first(n):
                x2[0:R, block(n)] = (dot_nt(zbuf[0:R], w[3, block(n), :]) + zbuf[R:2 * R, block(n)].astype(F32)).astype(BF)

            def second(n):
                x2[R:2 * R, block(n)] = (dot_nn(x2[0:R], wt[1, :, block(n)]) + vterm[0:R, block(n)]).astype(BF)

            def third(n):
                state[n] = (dot_nn(x2[R:2 * R], wt[0, :, block(n)]) + vterm[R:2 * R, block(n)]).astype(BF)
                shift(n, 0, arrived, shift_recv, 1).start()
            loop(4, first)
            loop(4, second)
            loop(4, third)
            for k, device in ((1, 2), (2, 3)):
                for n in range(4):
                    shift(n, k, arrived, shift_recv, device).start()
        make_perm()
        set_x_blocks(state)
        exchange(3, packed(transpose_chunk, perm_chunk))

        @pl.when(y < 2)
        def _():
            def rest(d):
                q = (quarter + 1 + d) % 4
                w[2, block(q), :] = dot_nn(w[0, block(q), :], w[1]).astype(BF)
            loop(3, rest)
            transpose_w(1, 2)
            make_wp(2)
        collect(3)

        @pl.when(y < 2)
        def _():
            eterm[...] = zbuf[...].astype(F32)

        @pl.when(y == 2)
        def _():
            sent_final[...] = zbuf[...]

        @pl.when(y == 3)
        def _():
            final[...] = zbuf[...]

    @pl.when(is_b & (y < 3))
    def _():
        send_positions()

        @pl.when(y == 2)
        def _():
            core_d.wait_recv()
        send_rows(dbuf[1])
        eterm[0:R] = dbuf[1].astype(F32)

        @pl.when(y == 2)
        def _():
            core_c.wait_recv()
            transpose_w(1, 1)
        make_perm()
        make_wp(1)
        collect_rows(eterm)

        @pl.when(y == 0)
        def _():
            for k in range(4):
                share(k)

    @pl.when(is_b & (y == 3))
    def _():
        send_rows(dbuf[1])
        final[0:R] = dbuf[1]
        collect_rows(final)

    slot = jnp.where(is_a, 2, 1)
    ends = (y < 2) | (is_b & (y == 2))

    @pl.when(y == 0)
    def _():
        u_sent.wait_recv()
        set_x_blocks(u_in)
        exchange(1, packed(product_chunk(slot), wp_chunk))

        @pl.when(is_b)
        def _():
            shared.wait_recv()
            copy_core.start()
            transpose_w(2, 3)

    @pl.when(ends)
    def _():
        @pl.when((y > 0) | is_b)
        def _():
            shifted(0).wait_recv()

        @pl.when((y == 0) & is_b)
        def _():
            for n in range(4):
                x3[0:R, 256 * n:256 * (n + 1)] = arrived[n]
            loop(4, lambda n: d_in.__setitem__((slice(None), block(n)), dot_nn(x3[0:R], wt[2, :, block(n)]).astype(BF)))
            give_v.start()
            set_x(x2, d_in[...])

        @pl.when((y == 0) & is_a)
        def _():
            give_v.wait_recv()
            set_x(x2, d_in[...])

        @pl.when(y > 0)
        def _():
            set_x_blocks(arrived)
        exchange(2, packed(product_chunk(slot), wp_chunk))

        @pl.when(y == 0)
        def _():
            @pl.when(is_a)
            def _():
                copy_core.wait_recv()
                transpose_w(2, 3)
            collect(1)
            vterm[...] = zbuf[...].astype(F32)
        collect(2)

        @pl.when(y == 0)
        def _():
            loop(4, lambda n: x3.__setitem__(
                (slice(None), block(n)), (dot_nn(zbuf[...], wt[2, :, block(n)]) + vterm[:, block(n)]).astype(BF)))
            zbuf[...] = x3[...]
        out = (eterm[...] + dot_nn(zbuf[...], wt[1])).astype(BF)

        @pl.when(y < 2)
        def _():
            final[...] = out

        @pl.when(y == 2)
        def _():
            sent_final[...] = out

    @pl.when(y == 2)
    def _():
        swap = remote(sent_final, final, swap_send, swap_recv, partner)
        swap.start()
        swap.wait()

    sigma_ref[...] = final[0:R]
    load_b.wait()
    column = lax.broadcasted_iota(jnp.int32, (1, N), 1) // 128
    chosen = jnp.zeros((1, N), jnp.int32)
    for n in range(pattern_ref.shape[1]):
        chosen = jnp.where(column == pattern[0, n], 1, chosen)
    masked = jnp.where(chosen == 1, final[R:2 * R].astype(F32), 0.0).astype(BF)
    grad_ref[...] = dot_nn(masked, basis[...]).astype(BF)

    when(gives_d, core_d.wait_send)
    when(gives_c, core_c.wait_send)
    when((y == 0) & is_b, copy_core.wait_send)
    when(is_b, rows_sent.wait_send)
    when(is_a | (y < 3), positions.wait_send)
    when(is_a, exchanged(0).wait_send)
    when((is_a & (y == 2)) | (y == 0), exchanged(1).wait_send)
    when(ends, exchanged(2).wait_send)
    when(is_a, exchanged(3).wait_send)
    when(is_a & (y > 0), shifted(0).wait_send)
    when(is_a & ((y == 1) | (y == 2)), shifted(1).wait_send)
    when(is_a & (y == 2), shifted(2).wait_send)
    when(is_b & (y == 0), give_v.wait_send)
    when(is_a & (y == 3), u_sent.wait_send)
    when(is_a & (y == 3), d_sent.wait_send)
    when(is_a & ((y == 3) | (y == 1)), parts_sent(0).wait_send)
    when((is_a & (y == 2)) | (is_b & (y == 0)), shared.wait_send)


def on_device(dinv, coupling, owner_position, pattern, basis):
    vmem = pl.BlockSpec(memory_space=pltpu.VMEM)
    hbm = pl.BlockSpec(memory_space=pltpu.HBM)
    h = basis.shape[1]
    dma = pltpu.SemaphoreType.DMA
    operands = (dinv[0], coupling[0], owner_position[None], pattern, basis)
    sigma, gradient = pl.pallas_call(
        kernel,
        out_shape=(jax.ShapeDtypeStruct((R, N), BF), jax.ShapeDtypeStruct((R, h), BF)),
        in_specs=[hbm] * len(operands),
        out_specs=(vmem, vmem),
        scratch_shapes=[
            pltpu.VMEM((4, N, N), BF),
            pltpu.VMEM((3, N, N), BF),
            pltpu.VMEM((N, N), BF),
            pltpu.VMEM((N, N), BF),
            pltpu.VMEM((2 * R, N), BF),
            pltpu.VMEM((2 * R, N), BF),
            pltpu.VMEM((2 * R, N), BF),
            pltpu.VMEM((2, R, N), BF),
            pltpu.VMEM((2 * R, N), F32),
            pltpu.VMEM((2 * R, N), F32),
            pltpu.VMEM((4, R, 256), BF),
            pltpu.VMEM((4, R, 256), BF),
            pltpu.VMEM((4, R, 256), BF),
            pltpu.VMEM((4, R, 256), BF),
            pltpu.VMEM((R, N), BF),
            pltpu.VMEM((2 * R, N), BF),
            pltpu.VMEM((2 * R, N), BF),
            pltpu.VMEM((N, h), BF),
            pltpu.VMEM((1, R), jnp.int32),
            pltpu.VMEM((8, 128), jnp.int32),
            pltpu.VMEM((SP, 8, 128), jnp.int32),
            pltpu.SMEM((1, 4), jnp.int32),
            pltpu.VMEM((4, SP, 2, 32, 128), BF),
            pltpu.VMEM((4, SP, 2, 32, 128), BF),
            pltpu.VMEM((SP, 16, 256), BF),
            pltpu.VMEM((SP, 16, 256), BF),
            dma((5,)), dma((3,)), dma((3,)), dma((4,)), dma, dma((2,)), dma, dma, dma((4,)), dma((4,)),
            dma, dma, dma, dma, dma, dma, dma, dma((4,)), dma, dma,
        ],
        compiler_params=pltpu.CompilerParams(
            collective_id=0, has_side_effects=True, vmem_limit_bytes=48 << 20),
        name="selected_inverse",
    )(*[pltpu.with_memory_space_constraint(a, pltpu.HBM) for a in operands])
    return sigma[None], gradient[None]


def solution(mesh):
    placed = (P("tm", "space", None), P("tm", None, None), P("space"), P("space", None), P())
    return jax.shard_map(
        on_device,
        mesh=mesh,
        in_specs=placed,
        out_specs=(P("tm", "space", None), P("tm", "space", None)),
        check_vma=False,
    )
```

```python
import jax
import jax.numpy as jnp
from jax import lax
from jax.experimental import pallas as pl
from jax.experimental.pallas import tpu as pltpu
from jax.sharding import PartitionSpec as P

MESH = pl.DeviceIdType.MESH
N = 1024
R = 64
SP = 16
F32 = jnp.float32
BF = jnp.bfloat16
FAR_FIRST = (10, 6, 14, 2, 9, 11, 5, 7, 13, 15, 1, 3, 8, 4, 12)


def dot_nt(a, b):
    return lax.dot_general(a, b, (((1,), (1,)), ((), ())), preferred_element_type=F32)


def dot_nn(a, b):
    return jnp.dot(a, b, preferred_element_type=F32)


def kernel(
    dinv_ref, coupling_ref, pos_ref, pattern_ref, basis_ref,
    sigma_ref, grad_ref,
    w, wt, wp, perm, x2, x3, zbuf, dbuf, eterm, vterm, state, arrived, u_out, u_in, d_in, sent_final, final, basis,
    pos, pos_out, pos_in, pattern, pieces_out, pieces_in, rows_out, rows_in,
    local_sem, core_send, core_recv, shift_send, shift_recv, u_send, u_recv, d_recv, ex_send, ex_recv,
    rows_send, rows_recv, swap_send, swap_recv, pos_send, pos_recv, part_send, part_recv, share_send, share_recv,
):
    tm, sp = lax.axis_index("tm"), lax.axis_index("space")
    y, c = tm // 2, tm % 2
    zc, xc = sp // 4, sp % 4
    partner = (y * 2 + 1 - c, sp)
    is_a = c == jnp.where(y == 2, 1, 0)
    is_b = jnp.logical_not(is_a)
    quarter = (zc % 2) * 2 + xc % 2

    def when(condition, work):
        pl.when(condition)(work)

    def loop(count, work):
        for index in range(count):
            work(index)

    def block(index, size=256):
        if isinstance(index, int):
            return slice(size * index, size * (index + 1))
        return pl.ds(pl.multiple_of(size * index, size), size)

    def remote(src, dst, send, recv, device):
        return pltpu.make_async_remote_copy(
            src_ref=src, dst_ref=dst, send_sem=send, recv_sem=recv, device_id=device, device_id_type=MESH)

    load_d = pltpu.make_async_copy(dinv_ref, dbuf.at[c], local_sem.at[0])
    load_c = pltpu.make_async_copy(coupling_ref, w.at[c], local_sem.at[1])
    load_p = pltpu.make_async_copy(pos_ref, pos, local_sem.at[2])
    load_t = pltpu.make_async_copy(pattern_ref, pattern, local_sem.at[3])
    load_b = pltpu.make_async_copy(basis_ref, basis, local_sem.at[4])
    for load in (load_c, load_d, load_p, load_t, load_b):
        load.start()

    barrier = pltpu.get_barrier_semaphore()

    def greet(t, s):
        pl.semaphore_signal(barrier, inc=1, device_id=(t, s), device_id_type=MESH)

    for d in FAR_FIRST:
        greet(tm, (sp + d) % SP)
    for dy in (2, 1, 3):
        for core in (0, 1):
            greet(((y + dy) % 4) * 2 + core, sp)
    greet(*partner)

    crossing = (tm == 5) | (tm == 7)

    @pl.when(crossing)
    def _():
        for d in FAR_FIRST:
            greet(12 - tm, (sp + d) % SP)

    lane = lax.broadcasted_iota(jnp.int32, (1, 1, 128), 2)
    low = lane < R
    lo = low[0]
    pick = low != (sp % 2 == 1)
    pick2 = pick[0]
    ri = lax.broadcasted_iota(jnp.int32, (256, 256), 0)
    ci = lax.broadcasted_iota(jnp.int32, (256, 256), 1)
    eye = (ri == ci).astype(BF)

    def transpose_w(to, slot):
        loop(4, lambda p: wt.__setitem__((to, slice(None), block(p)), w[slot, block(p), :].T))

    load_c.wait()
    when((c == 0) & (y != 2), lambda: transpose_w(0, 0))
    when((c == 1) & (y < 3), lambda: transpose_w(1, 1))
    load_d.wait()
    load_p.wait()
    load_t.wait()
    pl.semaphore_wait(barrier, SP + 6 + jnp.where(crossing, SP - 1, 0))

    core_d = remote(dbuf.at[c], dbuf.at[c], core_send.at[0], core_recv.at[0], partner)
    core_c = remote(w.at[c], w.at[c], core_send.at[1], core_recv.at[1], partner)
    copy_core = remote(w.at[3], w.at[3], core_send.at[2], core_recv.at[2], partner)
    gives_d = (c == 1) | (y == 2)
    gives_c = ((c == 1) & (y < 3)) | ((c == 0) & (y > 1))

    def part(slot, k):
        rows = pl.ds(pl.multiple_of(256 * quarter + 64 * k, 64), 64)
        return remote(w.at[slot, rows], w.at[3, rows], part_send, part_recv.at[k], (((y + 3) % 4) * 2 + 1, sp))

    def parts_sent(slot):
        return remote(w.at[slot, pl.ds(0, 256)], w.at[3, pl.ds(0, 256)], part_send, part_recv.at[0], partner)

    def share(k):
        part(3, k).wait_recv()
        first = 256 * quarter + 64 * k
        xs, zs = ((xc + 1) % 4, (xc + 3) % 4), ((zc + 1) % 4, (zc + 3) % 4)
        to = [(4 * zs[0] + xs[0], 0, 16), (4 * zs[0] + xs[1], 16, 16), (4 * zs[1] + xs[0], 32, 16), (4 * zs[1] + xs[1], 48, 16),
              (4 * zc + xs[0], 0, 32), (4 * zc + xs[1], 32, 32), (4 * zs[0] + xc, 0, 32), (4 * zs[1] + xc, 32, 32)]
        for device, offset, count in to:
            rows = pl.ds(pl.multiple_of(first + offset, 16), count)
            remote(w.at[3, rows], w.at[3, rows], share_send, share_recv, (tm, device)).start()

    shared = remote(w.at[3, pl.ds(0, 768)], w.at[3, pl.ds(0, 768)], share_send, share_recv, partner)

    def set_x(ref, value):
        ref[0:R] = value
        ref[R:2 * R] = value

    def set_x_blocks(blocks):
        for n in range(4):
            for h in range(2):
                x2[R * h:R * (h + 1), 256 * n:256 * (n + 1)] = blocks[n]

    def exchange(k, make, to=None):
        for dz in (2, 1, 3, 0):
            q = (zc + dz) % 4
            make(q, pieces_out.at[k, pl.ds(4 * q, 4)])
            for dx in (2, 1, 3, 0):
                i = 4 * q + (xc + dx) % 4
                if dz or dx or to is not None:
                    remote(pieces_out.at[k, i], pieces_in.at[k, sp], ex_send.at[k], ex_recv.at[k],
                           (tm if to is None else to, i)).start()
        if to is None:
            pieces_in[k, pl.ds(sp, 1)] = pieces_out[k, pl.ds(sp, 1)]

    def exchanged(k, count=SP - 1):
        some = pl.ds(0, count)
        return remote(pieces_out.at[k, some], pieces_in.at[k, some], ex_send.at[k], ex_recv.at[k], partner)

    def packed(*chunks):
        def make(q, out):
            for h, chunk in enumerate(chunks):
                v = chunk(q).reshape(4, 2, 32, 128)
                out[:, h] = jnp.where(pick, v[:, 0], v[:, 1]).astype(BF)
        return make

    def paired(chunk):
        def make(q, out):
            out[...] = chunk(q).reshape(4, 2, 32, 128).astype(BF)
        return make

    def collect(k, pair=False, count=SP - 1):
        exchanged(k, count).wait_recv()

        def columns(m):
            for h in range(2):
                a = pieces_in[k, 2 * m, h].astype(F32)
                b = pieces_in[k, 2 * m + 1, h].astype(F32)
                one, two = (32 * h, R + 32 * h) if pair else (R * h, R * h + 32)
                zbuf[one:one + 32, block(m, 128)] = jnp.where(lo, a, b).astype(BF)
                zbuf[two:two + 32, block(m, 128)] = pltpu.roll(jnp.where(lo, b, a), R, 1).astype(BF)
        loop(8, columns)

    def product_chunk(slot):
        return lambda q: dot_nt(w[slot, block(q), :], x2[...])

    def transpose_chunk(q):
        return dot_nt(eye, x2[:, block(q)])

    def perm_chunk(q):
        return dot_nt(perm[block(q), :], x2[...])

    def wp_chunk(q):
        return dot_nt(wp[block(q), :], x2[...])

    def level_chunk(q):
        return jnp.where(pick2, dot_nt(w[0, block(q), :], x2[...]), dot_nt(eye, x3[:, block(q)]))

    def send_positions():
        pos_out[...] = jnp.broadcast_to(jnp.concatenate([pos[...], pos[...]], axis=1), (8, 128))
        for d in FAR_FIRST:
            remote(pos_out, pos_in.at[sp], pos_send, pos_recv, (tm, (sp + d) % SP)).start()
        pos_in[pl.ds(sp, 1)] = pos_out[...][None]

    positions = remote(pos_in.at[pl.ds(0, SP - 1)], pos_in.at[pl.ds(0, SP - 1)], pos_send, pos_recv, partner)

    def make_perm():
        positions.wait_recv()
        p_index = lax.broadcasted_iota(jnp.int32, (N, 128), 0)

        def columns(m):
            row = jnp.where(lo, pos_in[2 * m, 0:1], pos_in[2 * m + 1, 0:1])
            perm[:, block(m, 128)] = (p_index == row).astype(BF)
        loop(8, columns)

    def make_wp(slot):
        loop(4, lambda p: wp.__setitem__((block(p), slice(None)), dot_nn(perm[block(p), :], w[slot]).astype(BF)))

    def send_rows(value):
        position = pos[...]
        target = position // R * 4 + position % 4
        place = (lax.broadcasted_iota(jnp.int32, (R, R), 0) == target).astype(BF)
        ordered = dot_nn(place, value).astype(BF)
        stacked = jnp.concatenate([ordered[:, 256 * k:256 * (k + 1)] for k in range(4)], axis=0)
        spread = (ci == (ri % 16) // 4 * R + ri // 16 * 4 + ri % 4).astype(BF)
        rows_out[...] = dot_nn(spread, stacked).astype(BF).reshape(SP, 16, 256)
        for d in FAR_FIRST:
            i = (sp + d) % SP
            remote(rows_out.at[i], rows_in.at[sp], rows_send, rows_recv, (tm, i)).start()
        rows_in[pl.ds(sp, 1)] = rows_out[pl.ds(sp, 1)]

    rows_sent = remote(rows_out.at[pl.ds(0, SP - 1)], rows_in.at[pl.ds(0, SP - 1)], rows_send, rows_recv, partner)

    def collect_rows(ref):
        rows_sent.wait_recv()
        gather = (ci == (ri % R) // 4 * 16 + ri // R * 4 + ri % 4).astype(BF)
        own = dot_nn(gather, rows_in[...].reshape(256, 256))
        for k in range(4):
            ref[R:2 * R, 256 * k:256 * (k + 1)] = own[R * k:R * (k + 1)].astype(ref.dtype)

    def shift(n, k, ref, recv, device):
        return remote(state.at[n], ref.at[n], shift_send.at[k], recv, (device, sp))

    def shifted(k):
        return remote(state, arrived, shift_send.at[k], shift_recv, partner)

    u_sent = remote(u_out, u_in, u_send.at[0], u_recv, (5, sp))
    d_sent = remote(dbuf.at[0], d_in, u_send.at[1], d_recv, (5, sp))

    give_u = remote(u_in, u_in, u_send.at[0], u_recv, partner)
    give_v = remote(d_in, d_in, u_send.at[1], d_recv, partner)
    when(gives_d, core_d.start)
    when(gives_c, core_c.start)

    @pl.when(is_a)
    def _():
        @pl.when(y == 3)
        def _():
            d_sent.start()
        core_d.wait_recv()

        @pl.when(y == 3)
        def _():
            def columns(n):
                u_out[n] = dot_nn(dbuf[1], wt[0, :, block(n)]).astype(BF)
                remote(u_out.at[n], u_in.at[n], u_send.at[0], u_recv, (5, sp)).start()
            loop(4, columns)

        @pl.when(y == 2)
        def _():
            d_sent.wait_recv()
            u_sent.wait_recv()
            odd = sp % 2
            for n in range(4):
                x2[pl.ds(pl.multiple_of(R * odd, R), R), 256 * n:256 * (n + 1)] = u_in[n]
            x2[pl.ds(pl.multiple_of(R * (1 - odd), R), R), :] = d_in[...]
            x2[...] = dot_nn(x2[...], wt[1]).astype(BF)
            core_c.wait_recv()
            exchange(1, paired(product_chunk(0)), 7)
        set_x(x2, dbuf[1])
        set_x(x3, dbuf[0])
        exchange(0, paired(level_chunk))
        send_positions()
        when(y == 2, lambda: transpose_w(0, 0))

        @pl.when(y < 2)
        def _():
            core_c.wait_recv()
            w[2, block(quarter), :] = dot_nn(w[0, block(quarter), :], w[1]).astype(BF)

            @pl.when(y == 1)
            def _():
                for k in range(4):
                    part(2, k).start()
        collect(0, True)

        @pl.when(y != 2)
        def _():
            e = (dot_nn(zbuf[0:R], wt[0]) + zbuf[R:2 * R].astype(F32)).astype(BF)
            for n in range(4):
                state[n] = e[:, 256 * n:256 * (n + 1)]

            @pl.when(y == 3)
            def _():
                for n in range(4):
                    shift(n, 0, arrived, shift_recv, 4).start()

            @pl.when(y == 1)
            def _():
                for n in range(4):
                    shift(n, 0, u_in, u_recv, 1).start()

        @pl.when(y == 2)
        def _():
            vterm[...] = zbuf[...].astype(F32)
            make_perm()
            shifted(0).wait_recv()
            for n in range(4):
                x2[0:R, 256 * n:256 * (n + 1)] = arrived[n]
            x2[R:2 * R] = (dot_nn(x2[0:R], wt[1]) + vterm[0:R]).astype(BF)

            def third(n):
                state[n] = (dot_nn(x2[R:2 * R], wt[0, :, block(n)]) + vterm[R:2 * R, block(n)]).astype(BF)
                shift(n, 0, arrived, shift_recv, 1).start()
            loop(4, third)
            for k, device in ((1, 2), (2, 3)):
                for n in range(4):
                    shift(n, k, arrived, shift_recv, device).start()
        when(y != 2, make_perm)
        set_x_blocks(state)
        exchange(3, packed(transpose_chunk, perm_chunk))

        @pl.when(y < 2)
        def _():
            def rest(d):
                q = (quarter + 1 + d) % 4
                w[2, block(q), :] = dot_nn(w[0, block(q), :], w[1]).astype(BF)
            loop(3, rest)
            transpose_w(1, 2)
            make_wp(2)
        collect(3)

        @pl.when(y < 2)
        def _():
            eterm[...] = zbuf[...].astype(F32)

        @pl.when(y == 2)
        def _():
            sent_final[...] = zbuf[...]

        @pl.when(y == 3)
        def _():
            final[...] = zbuf[...]

    @pl.when(is_b & (y < 3))
    def _():
        send_positions()

        @pl.when(y == 2)
        def _():
            core_d.wait_recv()
        send_rows(dbuf[1])
        eterm[0:R] = dbuf[1].astype(F32)

        @pl.when(y == 2)
        def _():
            core_c.wait_recv()
            transpose_w(1, 1)
        make_perm()
        make_wp(1)
        collect_rows(eterm)

        @pl.when(y == 0)
        def _():
            for k in range(4):
                share(k)

    @pl.when(is_b & (y == 3))
    def _():
        send_rows(dbuf[1])
        core_c.wait_recv()
        transpose_w(0, 0)
        final[0:R] = dbuf[1]
        collect_rows(final)
        collect(1, True, SP)
        t = (dot_nn(zbuf[0:R], wt[0]) + zbuf[R:2 * R].astype(F32)).astype(BF)
        for n in range(4):
            state[n] = t[:, 256 * n:256 * (n + 1)]
            shift(n, 0, arrived, shift_recv, 5).start()

    slot = jnp.where(is_a, 2, 1)
    ends = (y < 2) | (is_b & (y == 2))

    @pl.when(y == 0)
    def _():
        @pl.when(is_b)
        def _():
            u_sent.wait_recv()
            give_u.start()

        @pl.when(is_a)
        def _():
            give_u.wait_recv()
        set_x_blocks(u_in)
        exchange(1, packed(product_chunk(slot), wp_chunk))

        @pl.when(is_b)
        def _():
            shared.wait_recv()
            copy_core.start()
            transpose_w(2, 3)

    @pl.when(ends)
    def _():
        @pl.when((y > 0) | is_b)
        def _():
            shifted(0).wait_recv()

        @pl.when((y == 0) & is_b)
        def _():
            for n in range(4):
                x3[0:R, 256 * n:256 * (n + 1)] = arrived[n]
            d_in[...] = dot_nn(x3[0:R], wt[2]).astype(BF)
            give_v.start()
            set_x(x2, d_in[...])

        @pl.when((y == 0) & is_a)
        def _():
            give_v.wait_recv()
            set_x(x2, d_in[...])

        @pl.when(y > 0)
        def _():
            set_x_blocks(arrived)
        exchange(2, packed(product_chunk(slot), wp_chunk))

        @pl.when(y == 0)
        def _():
            @pl.when(is_a)
            def _():
                copy_core.wait_recv()
                transpose_w(2, 3)
            collect(1)
            vterm[...] = zbuf[...].astype(F32)
        collect(2)

        @pl.when(y == 0)
        def _():
            zbuf[...] = (dot_nn(zbuf[...], wt[2]) + vterm[...]).astype(BF)
        out = (eterm[...] + dot_nn(zbuf[...], wt[1])).astype(BF)

        @pl.when(y < 2)
        def _():
            final[...] = out

        @pl.when(y == 2)
        def _():
            sent_final[...] = out

    @pl.when(y == 2)
    def _():
        swap = remote(sent_final, final, swap_send, swap_recv, partner)
        swap.start()
        swap.wait()

    sigma_ref[...] = final[0:R]
    load_b.wait()
    column = lax.broadcasted_iota(jnp.int32, (1, N), 1) // 128
    chosen = jnp.zeros((1, N), jnp.int32)
    for n in range(pattern_ref.shape[1]):
        chosen = jnp.where(column == pattern[0, n], 1, chosen)
    masked = jnp.where(chosen == 1, final[R:2 * R].astype(F32), 0.0).astype(BF)
    grad_ref[...] = dot_nn(masked, basis[...]).astype(BF)

    when(gives_d, core_d.wait_send)
    when(gives_c, core_c.wait_send)
    when((y == 0) & is_b, copy_core.wait_send)
    when(is_b, rows_sent.wait_send)
    when(is_a | (y < 3), positions.wait_send)
    when(is_a, exchanged(0).wait_send)
    when(y == 0, exchanged(1).wait_send)
    when(is_a & (y == 2), exchanged(1, SP).wait_send)
    when(ends, exchanged(2).wait_send)
    when(is_a, exchanged(3).wait_send)
    when((is_a & (y > 0)) | (is_b & (y == 3)), shifted(0).wait_send)
    when(is_a & (y == 2), shifted(1).wait_send)
    when(is_a & (y == 2), shifted(2).wait_send)
    when(is_b & (y == 0), give_v.wait_send)
    when(is_b & (y == 0), give_u.wait_send)
    when(is_a & (y == 3), u_sent.wait_send)
    when(is_a & (y == 3), d_sent.wait_send)
    when(is_a & (y == 1), parts_sent(0).wait_send)
    when(is_b & (y == 0), shared.wait_send)


def on_device(dinv, coupling, owner_position, pattern, basis):
    vmem = pl.BlockSpec(memory_space=pltpu.VMEM)
    hbm = pl.BlockSpec(memory_space=pltpu.HBM)
    h = basis.shape[1]
    dma = pltpu.SemaphoreType.DMA
    operands = (dinv[0], coupling[0], owner_position[None], pattern, basis)
    sigma, gradient = pl.pallas_call(
        kernel,
        out_shape=(jax.ShapeDtypeStruct((R, N), BF), jax.ShapeDtypeStruct((R, h), BF)),
        in_specs=[hbm] * len(operands),
        out_specs=(vmem, vmem),
        scratch_shapes=[
            pltpu.VMEM((4, N, N), BF),
            pltpu.VMEM((3, N, N), BF),
            pltpu.VMEM((N, N), BF),
            pltpu.VMEM((N, N), BF),
            pltpu.VMEM((2 * R, N), BF),
            pltpu.VMEM((2 * R, N), BF),
            pltpu.VMEM((2 * R, N), BF),
            pltpu.VMEM((2, R, N), BF),
            pltpu.VMEM((2 * R, N), F32),
            pltpu.VMEM((2 * R, N), F32),
            pltpu.VMEM((4, R, 256), BF),
            pltpu.VMEM((4, R, 256), BF),
            pltpu.VMEM((4, R, 256), BF),
            pltpu.VMEM((4, R, 256), BF),
            pltpu.VMEM((R, N), BF),
            pltpu.VMEM((2 * R, N), BF),
            pltpu.VMEM((2 * R, N), BF),
            pltpu.VMEM((N, h), BF),
            pltpu.VMEM((1, R), jnp.int32),
            pltpu.VMEM((8, 128), jnp.int32),
            pltpu.VMEM((SP, 8, 128), jnp.int32),
            pltpu.SMEM((1, 4), jnp.int32),
            pltpu.VMEM((4, SP, 2, 32, 128), BF),
            pltpu.VMEM((4, SP, 2, 32, 128), BF),
            pltpu.VMEM((SP, 16, 256), BF),
            pltpu.VMEM((SP, 16, 256), BF),
            dma((5,)), dma((3,)), dma((3,)), dma((4,)), dma, dma((2,)), dma, dma, dma((4,)), dma((4,)),
            dma, dma, dma, dma, dma, dma, dma, dma((4,)), dma, dma,
        ],
        compiler_params=pltpu.CompilerParams(
            collective_id=0, has_side_effects=True, vmem_limit_bytes=48 << 20),
        name="selected_inverse",
    )(*[pltpu.with_memory_space_constraint(a, pltpu.HBM) for a in operands])
    return sigma[None], gradient[None]


def solution(mesh):
    placed = (P("tm", "space", None), P("tm", None, None), P("space"), P("space", None), P())
    return jax.shard_map(
        on_device,
        mesh=mesh,
        in_specs=placed,
        out_specs=(P("tm", "space", None), P("tm", "space", None)),
        check_vma=False,
    )
```

```python
import jax
import jax.numpy as jnp
from jax import lax
from jax.experimental import pallas as pl
from jax.experimental.pallas import tpu as pltpu
from jax.sharding import PartitionSpec as P

MESH = pl.DeviceIdType.MESH
N = 1024
R = 64
SP = 16
F32 = jnp.float32
BF = jnp.bfloat16
FAR_FIRST = (10, 6, 14, 2, 9, 11, 5, 7, 13, 15, 1, 3, 8, 4, 12)


def dot_nt(a, b):
    return lax.dot_general(a, b, (((1,), (1,)), ((), ())), preferred_element_type=F32)


def dot_nn(a, b):
    return jnp.dot(a, b, preferred_element_type=F32)


def kernel(
    dinv_ref, coupling_ref, pos_ref, pattern_ref, basis_ref,
    sigma_ref, grad_ref,
    w, wt, wp, perm, x2, x3, zbuf, dbuf, eterm, vterm, state, arrived, u_out, u_in, d_in, sent_final, final, basis,
    pos, pos_out, pos_in, pattern, pieces_out, pieces_in, rows_out, rows_in,
    local_sem, core_send, core_recv, shift_send, shift_recv, u_send, u_recv, d_recv, ex_send, ex_recv,
    rows_send, rows_recv, swap_send, swap_recv, pos_send, pos_recv, part_send, part_recv, share_send, share_recv, part_in,
):
    tm, sp = lax.axis_index("tm"), lax.axis_index("space")
    y, c = tm // 2, tm % 2
    zc, xc = sp // 4, sp % 4
    partner = (y * 2 + 1 - c, sp)
    is_a = c == jnp.where(y == 2, 1, 0)
    is_b = jnp.logical_not(is_a)
    quarter = (zc % 2) * 2 + xc % 2

    def when(condition, work):
        pl.when(condition)(work)

    def loop(count, work):
        for index in range(count):
            work(index)

    def block(index, size=256):
        if isinstance(index, int):
            return slice(size * index, size * (index + 1))
        return pl.ds(pl.multiple_of(size * index, size), size)

    def remote(src, dst, send, recv, device):
        return pltpu.make_async_remote_copy(
            src_ref=src, dst_ref=dst, send_sem=send, recv_sem=recv, device_id=device, device_id_type=MESH)

    load_d = pltpu.make_async_copy(dinv_ref, dbuf.at[c], local_sem.at[0])
    load_c = pltpu.make_async_copy(coupling_ref, w.at[c], local_sem.at[1])
    load_p = pltpu.make_async_copy(pos_ref, pos, local_sem.at[2])
    load_t = pltpu.make_async_copy(pattern_ref, pattern, local_sem.at[3])
    load_b = pltpu.make_async_copy(basis_ref, basis, local_sem.at[4])
    for load in (load_c, load_d, load_p, load_t, load_b):
        load.start()

    barrier = pltpu.get_barrier_semaphore()

    def greet(t, s):
        pl.semaphore_signal(barrier, inc=1, device_id=(t, s), device_id_type=MESH)

    for d in FAR_FIRST:
        greet(tm, (sp + d) % SP)
    for dy in (2, 1, 3):
        for core in (0, 1):
            greet(((y + dy) % 4) * 2 + core, sp)
    greet(*partner)

    for left, right in ((4, 5), (5, 7)):
        @pl.when((tm == left) | (tm == right))
        def _():
            for d in FAR_FIRST:
                greet(left + right - tm, (sp + d) % SP)

    lane = lax.broadcasted_iota(jnp.int32, (1, 1, 128), 2)
    low = lane < R
    lo = low[0]
    pick = low != (sp % 2 == 1)
    pick2 = pick[0]
    ri = lax.broadcasted_iota(jnp.int32, (256, 256), 0)
    ci = lax.broadcasted_iota(jnp.int32, (256, 256), 1)
    eye = (ri == ci).astype(BF)

    def transpose_w(to, slot):
        loop(4, lambda p: wt.__setitem__((to, slice(None), block(p)), w[slot, block(p), :].T))

    load_c.wait()
    when((c == 0) & (y != 2), lambda: transpose_w(0, 0))
    when((c == 1) & (y < 3), lambda: transpose_w(1, 1))
    load_d.wait()
    load_p.wait()
    load_t.wait()
    crossings = jnp.where(tm == 5, 2, jnp.where((tm == 4) | (tm == 7), 1, 0))
    pl.semaphore_wait(barrier, SP + 6 + (SP - 1) * crossings)

    core_d = remote(dbuf.at[c], dbuf.at[c], core_send.at[0], core_recv.at[0], partner)
    core_c = remote(w.at[c], w.at[c], core_send.at[1], core_recv.at[1], partner)

    def core_part(turn):
        rows = block((zc + (2, 1, 3, 0)[turn]) % 4)
        return remote(w.at[c, rows], w.at[c, rows], core_send.at[1], part_in.at[turn], partner)

    def core_c_here():
        for turn in range(4):
            core_part(turn).wait_recv()

    copy_core = remote(w.at[3], w.at[3], core_send.at[2], core_recv.at[2], partner)
    core_q = remote(w.at[0, block(quarter)], w.at[0, block(quarter)], core_send.at[2], core_recv.at[2], partner)
    gives_d = (c == 1) | (y == 2)
    gives_c = ((c == 1) & (y < 3)) | ((c == 0) & (y > 1))

    def part(slot, k):
        rows = pl.ds(pl.multiple_of(256 * quarter + 64 * k, 64), 64)
        return remote(w.at[slot, rows], w.at[3, rows], part_send, part_recv.at[k], (((y + 3) % 4) * 2 + 1, sp))

    def parts_sent(slot):
        return remote(w.at[slot, pl.ds(0, 256)], w.at[3, pl.ds(0, 256)], part_send, part_recv.at[0], partner)

    def share(k):
        part(3, k).wait_recv()
        first = 256 * quarter + 64 * k
        xs, zs = ((xc + 1) % 4, (xc + 3) % 4), ((zc + 1) % 4, (zc + 3) % 4)
        to = [(4 * zs[0] + xs[0], 0, 16), (4 * zs[0] + xs[1], 16, 16), (4 * zs[1] + xs[0], 32, 16), (4 * zs[1] + xs[1], 48, 16),
              (4 * zc + xs[0], 0, 32), (4 * zc + xs[1], 32, 32), (4 * zs[0] + xc, 0, 32), (4 * zs[1] + xc, 32, 32)]
        for device, offset, count in to:
            rows = pl.ds(pl.multiple_of(first + offset, 16), count)
            remote(w.at[3, rows], w.at[3, rows], share_send, share_recv, (tm, device)).start()

    shared = remote(w.at[3, pl.ds(0, 768)], w.at[3, pl.ds(0, 768)], share_send, share_recv, partner)

    def set_x(ref, value):
        ref[0:R] = value
        ref[R:2 * R] = value

    def set_x_blocks(blocks):
        for n in range(4):
            for h in range(2):
                x2[R * h:R * (h + 1), 256 * n:256 * (n + 1)] = blocks[n]

    def piece(ref, k, i, single):
        return ref.at[k, i, 0] if single else ref.at[k, i]

    def exchange(k, make, to=None, single=False, into=None):
        for dz in (2, 1, 3, 0):
            q = (zc + dz) % 4
            make(q, pieces_out.at[k, pl.ds(4 * q, 4)])
            for dx in (2, 1, 3, 0):
                i = 4 * q + (xc + dx) % 4
                if dz or dx or to is not None:
                    slot = k if into is None else into
                    remote(piece(pieces_out, k, i, single), piece(pieces_in, slot, sp, single), ex_send.at[k], ex_recv.at[slot],
                           (tm if to is None else to, i)).start()
        if to is None:
            pieces_in[k, pl.ds(sp, 1)] = pieces_out[k, pl.ds(sp, 1)]

    def exchanged(k, count=SP - 1, single=False):
        some = pl.ds(0, count)
        return remote(piece(pieces_out, k, some, single), piece(pieces_in, k, some, single), ex_send.at[k], ex_recv.at[k], partner)

    def packed(*chunks):
        def make(q, out):
            for h, chunk in enumerate(chunks):
                v = chunk(q).reshape(4, 2, 32, 128)
                out[:, h] = jnp.where(pick, v[:, 0], v[:, 1]).astype(BF)
        return make

    def paired(chunk):
        def make(q, out):
            out[...] = chunk(q).reshape(4, 2, 32, 128).astype(BF)
        return make

    def collect(k, pair=False, count=SP - 1, single=False):
        exchanged(k, count, single).wait_recv()

        def columns(m):
            for h in range(1 if single else 2):
                a = pieces_in[k, 2 * m, h].astype(F32)
                b = pieces_in[k, 2 * m + 1, h].astype(F32)
                one, two = (32 * h, R + 32 * h) if pair else (R * h, R * h + 32)
                zbuf[one:one + 32, block(m, 128)] = jnp.where(lo, a, b).astype(BF)
                zbuf[two:two + 32, block(m, 128)] = pltpu.roll(jnp.where(lo, b, a), R, 1).astype(BF)
        loop(8, columns)

    def product_chunk(slot):
        return lambda q: dot_nt(w[slot, block(q), :], x2[...])

    def transpose_chunk(q):
        return dot_nt(eye, x2[:, block(q)])

    def perm_chunk(q):
        return dot_nt(perm[block(q), :], x2[...])

    def wp_chunk(q):
        return dot_nt(wp[block(q), :], x2[...])

    def level_chunk(q):
        return jnp.where(pick2, dot_nt(w[0, block(q), :], x2[...]), dot_nt(eye, x3[:, block(q)]))

    def send_positions():
        pos_out[...] = jnp.broadcast_to(jnp.concatenate([pos[...], pos[...]], axis=1), (8, 128))
        for d in FAR_FIRST:
            remote(pos_out, pos_in.at[sp], pos_send, pos_recv, (tm, (sp + d) % SP)).start()
        pos_in[pl.ds(sp, 1)] = pos_out[...][None]

    positions = remote(pos_in.at[pl.ds(0, SP - 1)], pos_in.at[pl.ds(0, SP - 1)], pos_send, pos_recv, partner)

    def make_perm():
        positions.wait_recv()
        p_index = lax.broadcasted_iota(jnp.int32, (N, 128), 0)

        def columns(m):
            row = jnp.where(lo, pos_in[2 * m, 0:1], pos_in[2 * m + 1, 0:1])
            perm[:, block(m, 128)] = (p_index == row).astype(BF)
        loop(8, columns)

    def make_wp(slot):
        loop(4, lambda p: wp.__setitem__((block(p), slice(None)), dot_nn(perm[block(p), :], w[slot]).astype(BF)))

    def send_rows(value):
        position = pos[...]
        target = position // R * 4 + position % 4
        place = (lax.broadcasted_iota(jnp.int32, (R, R), 0) == target).astype(BF)
        ordered = dot_nn(place, value).astype(BF)
        stacked = jnp.concatenate([ordered[:, 256 * k:256 * (k + 1)] for k in range(4)], axis=0)
        spread = (ci == (ri % 16) // 4 * R + ri // 16 * 4 + ri % 4).astype(BF)
        rows_out[...] = dot_nn(spread, stacked).astype(BF).reshape(SP, 16, 256)
        for d in FAR_FIRST:
            i = (sp + d) % SP
            remote(rows_out.at[i], rows_in.at[sp], rows_send, rows_recv, (tm, i)).start()
        rows_in[pl.ds(sp, 1)] = rows_out[pl.ds(sp, 1)]

    rows_sent = remote(rows_out.at[pl.ds(0, SP - 1)], rows_in.at[pl.ds(0, SP - 1)], rows_send, rows_recv, partner)

    def collect_rows(ref):
        rows_sent.wait_recv()
        gather = (ci == (ri % R) // 4 * 16 + ri // R * 4 + ri % 4).astype(BF)
        own = dot_nn(gather, rows_in[...].reshape(256, 256))
        for k in range(4):
            ref[R:2 * R, 256 * k:256 * (k + 1)] = own[R * k:R * (k + 1)].astype(ref.dtype)

    def shift(n, k, ref, recv, device):
        return remote(state.at[n], ref.at[n], shift_send.at[k], recv.at[n], (device, sp))

    def shifted(k):
        return remote(state, arrived, shift_send.at[k], shift_recv.at[0], partner)

    def arrive(n):
        remote(state.at[n], arrived.at[n], shift_send.at[0], shift_recv.at[n], partner).wait_recv()

    def u_arrive(n):
        remote(u_out.at[n], u_in.at[n], u_send.at[0], u_recv.at[n], partner).wait_recv()

    u_sent = remote(u_out, u_in, u_send.at[0], u_recv.at[0], (5, sp))
    d_sent = remote(dbuf.at[0], d_in, u_send.at[1], d_recv, (4, sp))

    give_u = remote(u_in, u_in, u_send.at[0], u_recv.at[0], partner)
    give_v = remote(d_in, d_in, u_send.at[1], d_recv, partner)
    when(is_a & (y == 1), core_q.start)
    when(gives_d, core_d.start)

    @pl.when(gives_c)
    def _():
        for turn in range(4):
            core_part(turn).start()

    @pl.when(is_a)
    def _():
        core_d.wait_recv()

        @pl.when(y == 3)
        def _():
            def columns(n):
                u_out[n] = dot_nn(dbuf[1], wt[0, :, block(n)]).astype(BF)
                remote(u_out.at[n], u_in.at[n], u_send.at[0], u_recv.at[n], (5, sp)).start()
            loop(4, columns)
            d_sent.start()

        @pl.when(y == 2)
        def _():
            total = None
            for n in range(4):
                u_arrive(n)
                term = dot_nn(u_in[n], wt[1, block(n), :])
                total = term if total is None else total + term
            set_x(x2, total.astype(BF))
            turns = iter(range(4))

            def chunk(q):
                core_part(next(turns)).wait_recv()
                return product_chunk(0)(q)
            exchange(1, packed(chunk), 7, True)
        @pl.when(y != 2)
        def _():
            set_x(x2, dbuf[1])
            set_x(x3, dbuf[0])
            exchange(0, paired(level_chunk))
        send_positions()
        when(y == 2, lambda: transpose_w(0, 0))

        when(y < 2, core_c_here)

        @pl.when(y != 2)
        def _():
            collect(0, True)
            e = (dot_nn(zbuf[0:R], wt[0]) + zbuf[R:2 * R].astype(F32)).astype(BF)
            for n in range(4):
                state[n] = e[:, 256 * n:256 * (n + 1)]

            @pl.when(y == 3)
            def _():
                for n in range(4):
                    shift(n, 0, arrived, shift_recv, 4).start()

            @pl.when(y == 1)
            def _():
                for n in range(4):
                    shift(n, 0, u_in, u_recv, 1).start()

        @pl.when(y == 2)
        def _():
            collect(0, True, SP)
            vterm[...] = zbuf[...].astype(F32)
            collect(2, False, SP, True)
            total = vterm[0:R]
            for n in range(4):
                arrive(n)
                t = (arrived[n].astype(F32) + zbuf[0:R, block(n)].astype(F32)).astype(BF)
                total = total + dot_nn(t, wt[1, block(n), :])
            x2[R:2 * R] = total.astype(BF)

            def third(n):
                state[n] = (dot_nn(x2[R:2 * R], wt[0, :, block(n)]) + vterm[R:2 * R, block(n)]).astype(BF)
                shift(n, 0, arrived, shift_recv, 1).start()
            loop(4, third)
            for k, device in ((1, 2), (2, 3)):
                for n in range(4):
                    shift(n, k, arrived, shift_recv, device).start()
        make_perm()
        set_x_blocks(state)
        exchange(3, packed(transpose_chunk, perm_chunk))

        @pl.when(y < 2)
        def _():
            def rows(q):
                w[2, block(q), :] = dot_nn(w[0, block(q), :], w[1]).astype(BF)
            loop(4, rows)
            transpose_w(1, 2)
            make_wp(2)
        collect(3)

        @pl.when(y < 2)
        def _():
            eterm[...] = zbuf[...].astype(F32)

        @pl.when(y == 2)
        def _():
            sent_final[...] = zbuf[...]

        @pl.when(y == 3)
        def _():
            final[...] = zbuf[...]

    @pl.when(is_b & (y < 3))
    def _():
        @pl.when(y == 2)
        def _():
            core_d.wait_recv()
            set_x(x2, dbuf[1])
            set_x(x3, dbuf[0])
            exchange(0, paired(level_chunk), 5)
        send_positions()
        send_rows(dbuf[1])

        @pl.when(y == 1)
        def _():
            core_q.wait_recv()
            w[2, block(quarter), :] = dot_nn(w[0, block(quarter), :], w[1]).astype(BF)
            for k in range(4):
                part(2, k).start()
        eterm[0:R] = dbuf[1].astype(F32)

        @pl.when(y == 2)
        def _():
            core_c_here()
            transpose_w(1, 1)
            d_sent.wait_recv()
            set_x(x2, dot_nn(d_in[...], wt[1]).astype(BF))
            exchange(1, packed(product_chunk(0)), 5, True, 2)
        make_perm()
        for k in range(4):
            when(y == 0, lambda: share(k))
            wp[block(k), :] = dot_nn(perm[block(k), :], w[1]).astype(BF)
        collect_rows(eterm)

    @pl.when(is_b & (y == 3))
    def _():
        send_rows(dbuf[1])
        core_c_here()
        transpose_w(0, 0)
        final[0:R] = dbuf[1]
        collect_rows(final)
        collect(1, False, SP, True)
        for n in range(4):
            state[n] = dot_nn(zbuf[0:R], wt[0, :, block(n)]).astype(BF)
            shift(n, 0, arrived, shift_recv, 5).start()

    slot = jnp.where(is_a, 2, 1)
    ends = (y < 2) | (is_b & (y == 2))

    @pl.when(y == 0)
    def _():
        @pl.when(is_b)
        def _():
            loop(4, u_arrive)
            give_u.start()

        @pl.when(is_a)
        def _():
            give_u.wait_recv()
        set_x_blocks(u_in)
        exchange(1, packed(product_chunk(slot), wp_chunk))

        @pl.when(is_b)
        def _():
            shared.wait_recv()
            copy_core.start()
            transpose_w(2, 3)

    @pl.when(ends)
    def _():
        @pl.when((y == 0) & is_b)
        def _():
            total = None
            for n in range(4):
                arrive(n)
                term = dot_nn(arrived[n], wt[2, block(n), :])
                total = term if total is None else total + term
            d_in[...] = total.astype(BF)
            give_v.start()
            set_x(x2, d_in[...])

        @pl.when((y == 0) & is_a)
        def _():
            give_v.wait_recv()
            set_x(x2, d_in[...])

        @pl.when(y > 0)
        def _():
            loop(4, arrive)
            set_x_blocks(arrived)
        exchange(2, packed(product_chunk(slot), wp_chunk))

        @pl.when(y == 0)
        def _():
            @pl.when(is_a)
            def _():
                copy_core.wait_recv()
                transpose_w(2, 3)
            collect(1)
            vterm[...] = zbuf[...].astype(F32)
        collect(2)

        @pl.when(y == 0)
        def _():
            zbuf[...] = (dot_nn(zbuf[...], wt[2]) + vterm[...]).astype(BF)
        out = (eterm[...] + dot_nn(zbuf[...], wt[1])).astype(BF)

        @pl.when(y < 2)
        def _():
            final[...] = out

        @pl.when(y == 2)
        def _():
            sent_final[...] = out

    @pl.when(y == 2)
    def _():
        swap = remote(sent_final, final, swap_send, swap_recv, partner)
        swap.start()
        swap.wait()

    sigma_ref[...] = final[0:R]
    load_b.wait()
    column = lax.broadcasted_iota(jnp.int32, (1, N), 1) // 128
    chosen = jnp.zeros((1, N), jnp.int32)
    for n in range(pattern_ref.shape[1]):
        chosen = jnp.where(column == pattern[0, n], 1, chosen)
    masked = jnp.where(chosen == 1, final[R:2 * R].astype(F32), 0.0).astype(BF)
    grad_ref[...] = dot_nn(masked, basis[...]).astype(BF)

    when(gives_d, core_d.wait_send)
    when(gives_c, core_c.wait_send)
    when((y == 0) & is_b, copy_core.wait_send)
    when(is_b, rows_sent.wait_send)
    when(is_a | (y < 3), positions.wait_send)
    when(is_a & (y != 2), exchanged(0).wait_send)
    when(is_b & (y == 2), exchanged(0, SP).wait_send)
    when(is_b & (y == 2), exchanged(1, SP, True).wait_send)
    when(y == 0, exchanged(1).wait_send)
    when(is_a & (y == 2), exchanged(1, SP, True).wait_send)
    when(ends, exchanged(2).wait_send)
    when(is_a, exchanged(3).wait_send)
    when((is_a & (y > 0)) | (is_b & (y == 3)), shifted(0).wait_send)
    when(is_a & (y == 2), shifted(1).wait_send)
    when(is_a & (y == 2), shifted(2).wait_send)
    when(is_b & (y == 0), give_v.wait_send)
    when(is_b & (y == 0), give_u.wait_send)
    when(is_a & (y == 3), u_sent.wait_send)
    when(is_a & (y == 3), d_sent.wait_send)
    when(is_b & (y == 1), parts_sent(0).wait_send)
    when(is_a & (y == 1), core_q.wait_send)
    when(is_b & (y == 0), shared.wait_send)


def on_device(dinv, coupling, owner_position, pattern, basis):
    vmem = pl.BlockSpec(memory_space=pltpu.VMEM)
    hbm = pl.BlockSpec(memory_space=pltpu.HBM)
    h = basis.shape[1]
    dma = pltpu.SemaphoreType.DMA
    operands = (dinv[0], coupling[0], owner_position[None], pattern, basis)
    sigma, gradient = pl.pallas_call(
        kernel,
        out_shape=(jax.ShapeDtypeStruct((R, N), BF), jax.ShapeDtypeStruct((R, h), BF)),
        in_specs=[hbm] * len(operands),
        out_specs=(vmem, vmem),
        scratch_shapes=[
            pltpu.VMEM((4, N, N), BF),
            pltpu.VMEM((3, N, N), BF),
            pltpu.VMEM((N, N), BF),
            pltpu.VMEM((N, N), BF),
            pltpu.VMEM((2 * R, N), BF),
            pltpu.VMEM((2 * R, N), BF),
            pltpu.VMEM((2 * R, N), BF),
            pltpu.VMEM((2, R, N), BF),
            pltpu.VMEM((2 * R, N), F32),
            pltpu.VMEM((2 * R, N), F32),
            pltpu.VMEM((4, R, 256), BF),
            pltpu.VMEM((4, R, 256), BF),
            pltpu.VMEM((4, R, 256), BF),
            pltpu.VMEM((4, R, 256), BF),
            pltpu.VMEM((R, N), BF),
            pltpu.VMEM((2 * R, N), BF),
            pltpu.VMEM((2 * R, N), BF),
            pltpu.VMEM((N, h), BF),
            pltpu.VMEM((1, R), jnp.int32),
            pltpu.VMEM((8, 128), jnp.int32),
            pltpu.VMEM((SP, 8, 128), jnp.int32),
            pltpu.SMEM((1, 4), jnp.int32),
            pltpu.VMEM((4, SP, 2, 32, 128), BF),
            pltpu.VMEM((4, SP, 2, 32, 128), BF),
            pltpu.VMEM((SP, 16, 256), BF),
            pltpu.VMEM((SP, 16, 256), BF),
            dma((5,)), dma((3,)), dma((3,)), dma((4,)), dma((4,)), dma((2,)), dma((4,)), dma, dma((4,)), dma((4,)),
            dma, dma, dma, dma, dma, dma, dma, dma((4,)), dma, dma, dma((4,)),
        ],
        compiler_params=pltpu.CompilerParams(
            collective_id=0, has_side_effects=True, vmem_limit_bytes=48 << 20),
        name="selected_inverse",
    )(*[pltpu.with_memory_space_constraint(a, pltpu.HBM) for a in operands])
    return sigma[None], gradient[None]


def solution(mesh):
    placed = (P("tm", "space", None), P("tm", None, None), P("space"), P("space", None), P())
    return jax.shard_map(
        on_device,
        mesh=mesh,
        in_specs=placed,
        out_specs=(P("tm", "space", None), P("tm", "space", None)),
        check_vma=False,
    )
```

```python
import jax
import jax.numpy as jnp
from jax import lax
from jax.experimental import pallas as pl
from jax.experimental.pallas import tpu as pltpu
from jax.sharding import PartitionSpec as P

MESH = pl.DeviceIdType.MESH
N = 1024
R = 64
SP = 16
F32 = jnp.float32
BF = jnp.bfloat16
FAR_FIRST = (10, 6, 14, 2, 9, 11, 5, 7, 13, 15, 1, 3, 8, 4, 12)

ONE_TO_ONE = ((1, 0), (2, 1), (2, 3), (3, 1), (3, 2), (5, 1), (5, 2), (5, 3), (5, 4), (6, 4), (6, 5), (7, 5), (7, 6))
ALL_TO_ALL = tuple((t, t) for t in range(7)) + ((4, 5), (5, 7), (6, 7))


def dot_nt(a, b):
    return lax.dot_general(a, b, (((1,), (1,)), ((), ())), preferred_element_type=F32)


def dot_nn(a, b):
    return jnp.dot(a, b, preferred_element_type=F32)


def kernel(
    dinv_ref, coupling_ref, pos_ref, pattern_ref, basis_ref,
    sigma_ref, grad_ref,
    w, wt, wp, perm, x2, x3, zbuf, dbuf, eterm, vterm, state, arrived, u_out, u_in, d_in, sent_final, final, basis,
    pos, pos_out, pos_in, pattern, pieces_out, pieces_in, rows_out, rows_in,
    local_sem, core_send, core_recv, shift_send, shift_recv, u_send, u_recv, d_recv, ex_send, ex_recv,
    rows_send, rows_recv, swap_send, swap_recv, pos_send, pos_recv, part_send, part_recv, share_send, share_recv, part_in,
):
    tm, sp = lax.axis_index("tm"), lax.axis_index("space")
    y, c = tm // 2, tm % 2
    zc, xc = sp // 4, sp % 4
    partner = (y * 2 + 1 - c, sp)
    is_a = c == jnp.where(y == 2, 1, 0)
    is_b = jnp.logical_not(is_a)
    quarter = (zc % 2) * 2 + xc % 2

    def when(condition, work):
        pl.when(condition)(work)

    def loop(count, work):
        for index in range(count):
            work(index)

    def block(index, size=256):
        if isinstance(index, int):
            return slice(size * index, size * (index + 1))
        return pl.ds(pl.multiple_of(size * index, size), size)

    def remote(src, dst, send, recv, device):
        return pltpu.make_async_remote_copy(
            src_ref=src, dst_ref=dst, send_sem=send, recv_sem=recv, device_id=device, device_id_type=MESH)

    load_d = pltpu.make_async_copy(dinv_ref, dbuf.at[c], local_sem.at[0])
    load_c = pltpu.make_async_copy(coupling_ref, w.at[c], local_sem.at[1])
    load_p = pltpu.make_async_copy(pos_ref, pos, local_sem.at[2])
    load_t = pltpu.make_async_copy(pattern_ref, pattern, local_sem.at[3])
    load_b = pltpu.make_async_copy(basis_ref, basis, local_sem.at[4])
    for load in (load_d, load_c, load_p, load_t, load_b):
        load.start()

    barrier = pltpu.get_barrier_semaphore()

    def greet(t, s):
        pl.semaphore_signal(barrier, inc=1, device_id=(t, s), device_id_type=MESH)

    for t in range(8):
        @pl.when(tm == t)
        def _():
            for source, to in ALL_TO_ALL:
                if to == t:
                    for d in FAR_FIRST + ((0,) if source != to else ()):
                        greet(source, (sp + d) % SP)
            for source, to in ONE_TO_ONE:
                if to == t:
                    greet(source, sp)
    greets = sum(jnp.where(tm == t, sum(SP - (a == b) for a, b in ALL_TO_ALL if a == t) + sum(a == t for a, _ in ONE_TO_ONE), 0)
                 for t in range(8))

    lane = lax.broadcasted_iota(jnp.int32, (1, 1, 128), 2)
    low = lane < R
    lo = low[0]
    pick = low != (sp % 2 == 1)
    pick2 = pick[0]
    ri = lax.broadcasted_iota(jnp.int32, (256, 256), 0)
    ci = lax.broadcasted_iota(jnp.int32, (256, 256), 1)
    eye = (ri == ci).astype(BF)

    def transpose_w(to, slot):
        loop(4, lambda p: wt.__setitem__((to, slice(None), block(p)), w[slot, block(p), :].T))

    core_d = remote(dbuf.at[c], dbuf.at[c], core_send.at[0], core_recv.at[0], partner)
    load_d.wait()

    @pl.when(tm == 7)
    def _():
        pl.semaphore_wait(barrier, greets)
        core_d.start()
    load_c.wait()
    when((c == 0) & (y != 2), lambda: transpose_w(0, 0))
    when((c == 1) & (y < 3), lambda: transpose_w(1, 1))
    load_p.wait()
    load_t.wait()

    @pl.when(tm == 6)
    def _():
        core_d.wait_recv()
        for n in range(4):
            u_out[n] = dot_nn(dbuf[1], wt[0, :, block(n)]).astype(BF)

    @pl.when(tm != 7)
    def _():
        pl.semaphore_wait(barrier, greets)

    core_c = remote(w.at[c], w.at[c], core_send.at[1], core_recv.at[1], partner)

    def core_part(turn):
        rows = block((zc + (2, 1, 3, 0)[turn]) % 4)
        return remote(w.at[c, rows], w.at[c, rows], core_send.at[1], part_in.at[turn], partner)

    def core_c_here():
        for turn in range(4):
            core_part(turn).wait_recv()

    copy_core = remote(w.at[3], w.at[3], core_send.at[2], core_recv.at[2], partner)
    core_q = remote(w.at[0, block(quarter)], w.at[0, block(quarter)], core_send.at[2], core_recv.at[2], partner)
    gives_d = (c == 1) | (y == 2)
    gives_c = ((c == 1) & (y < 3)) | ((c == 0) & (y > 1))

    def part(slot, k):
        rows = pl.ds(pl.multiple_of(256 * quarter + 64 * k, 64), 64)
        return remote(w.at[slot, rows], w.at[3, rows], part_send, part_recv.at[k], (((y + 3) % 4) * 2 + 1, sp))

    def parts_sent(slot):
        return remote(w.at[slot, pl.ds(0, 256)], w.at[3, pl.ds(0, 256)], part_send, part_recv.at[0], partner)

    def share(k):
        part(3, k).wait_recv()
        first = 256 * quarter + 64 * k
        xs, zs = ((xc + 1) % 4, (xc + 3) % 4), ((zc + 1) % 4, (zc + 3) % 4)
        to = [(4 * zs[0] + xs[0], 0, 16), (4 * zs[0] + xs[1], 16, 16), (4 * zs[1] + xs[0], 32, 16), (4 * zs[1] + xs[1], 48, 16),
              (4 * zc + xs[0], 0, 32), (4 * zc + xs[1], 32, 32), (4 * zs[0] + xc, 0, 32), (4 * zs[1] + xc, 32, 32)]
        for device, offset, count in to:
            rows = pl.ds(pl.multiple_of(first + offset, 16), count)
            remote(w.at[3, rows], w.at[3, rows], share_send, share_recv, (tm, device)).start()

    shared = remote(w.at[3, pl.ds(0, 768)], w.at[3, pl.ds(0, 768)], share_send, share_recv, partner)

    def set_x(ref, value):
        ref[0:R] = value
        ref[R:2 * R] = value

    def set_x_blocks(blocks):
        for n in range(4):
            for h in range(2):
                x2[R * h:R * (h + 1), 256 * n:256 * (n + 1)] = blocks[n]

    def piece(ref, k, i, single):
        return ref.at[k, i, 0] if single else ref.at[k, i]

    def exchange(k, make, to=None, single=False, into=None):
        for dz in (2, 1, 3, 0):
            q = (zc + dz) % 4
            make(q, pieces_out.at[k, pl.ds(4 * q, 4)])
            for dx in (2, 1, 3, 0):
                i = 4 * q + (xc + dx) % 4
                if dz or dx or to is not None:
                    slot = k if into is None else into
                    remote(piece(pieces_out, k, i, single), piece(pieces_in, slot, sp, single), ex_send.at[k], ex_recv.at[slot],
                           (tm if to is None else to, i)).start()
        if to is None:
            pieces_in[k, pl.ds(sp, 1)] = pieces_out[k, pl.ds(sp, 1)]

    def exchanged(k, count=SP - 1, single=False):
        some = pl.ds(0, count)
        return remote(piece(pieces_out, k, some, single), piece(pieces_in, k, some, single), ex_send.at[k], ex_recv.at[k], partner)

    def packed(*chunks):
        def make(q, out):
            for h, chunk in enumerate(chunks):
                v = chunk(q).reshape(4, 2, 32, 128)
                out[:, h] = jnp.where(pick, v[:, 0], v[:, 1]).astype(BF)
        return make

    def paired(chunk):
        def make(q, out):
            out[...] = chunk(q).reshape(4, 2, 32, 128).astype(BF)
        return make

    def collect(k, pair=False, count=SP - 1, single=False):
        exchanged(k, count, single).wait_recv()

        def columns(m):
            for h in range(1 if single else 2):
                a = pieces_in[k, 2 * m, h].astype(F32)
                b = pieces_in[k, 2 * m + 1, h].astype(F32)
                one, two = (32 * h, R + 32 * h) if pair else (R * h, R * h + 32)
                zbuf[one:one + 32, block(m, 128)] = jnp.where(lo, a, b).astype(BF)
                zbuf[two:two + 32, block(m, 128)] = pltpu.roll(jnp.where(lo, b, a), R, 1).astype(BF)
        loop(8, columns)

    def product_chunk(slot):
        return lambda q: dot_nt(w[slot, block(q), :], x2[...])

    def transpose_chunk(q):
        return dot_nt(eye, x2[:, block(q)])

    def perm_chunk(q):
        return dot_nt(perm[block(q), :], x2[...])

    def wp_chunk(q):
        return dot_nt(wp[block(q), :], x2[...])

    def level_chunk(q):
        return jnp.where(pick2, dot_nt(w[0, block(q), :], x2[...]), dot_nt(eye, x3[:, block(q)]))

    def send_positions():
        pos_out[...] = jnp.broadcast_to(jnp.concatenate([pos[...], pos[...]], axis=1), (8, 128))
        for d in FAR_FIRST:
            remote(pos_out, pos_in.at[sp], pos_send, pos_recv, (tm, (sp + d) % SP)).start()
        pos_in[pl.ds(sp, 1)] = pos_out[...][None]

    positions = remote(pos_in.at[pl.ds(0, SP - 1)], pos_in.at[pl.ds(0, SP - 1)], pos_send, pos_recv, partner)

    def make_perm():
        positions.wait_recv()
        p_index = lax.broadcasted_iota(jnp.int32, (N, 128), 0)

        def columns(m):
            row = jnp.where(lo, pos_in[2 * m, 0:1], pos_in[2 * m + 1, 0:1])
            perm[:, block(m, 128)] = (p_index == row).astype(BF)
        loop(8, columns)

    def make_wp(slot):
        loop(4, lambda p: wp.__setitem__((block(p), slice(None)), dot_nn(perm[block(p), :], w[slot]).astype(BF)))

    def send_rows(value, to=None):
        position = pos[...]
        target = position // R * 4 + position % 4
        place = (lax.broadcasted_iota(jnp.int32, (R, R), 0) == target).astype(BF)
        ordered = dot_nn(place, value).astype(BF)
        stacked = jnp.concatenate([ordered[:, 256 * k:256 * (k + 1)] for k in range(4)], axis=0)
        spread = (ci == (ri % 16) // 4 * R + ri // 16 * 4 + ri % 4).astype(BF)
        rows_out[...] = dot_nn(spread, stacked).astype(BF).reshape(SP, 16, 256)
        for d in FAR_FIRST:
            i = (sp + d) % SP
            remote(rows_out.at[i], rows_in.at[sp], rows_send, rows_recv, (tm if to is None else to, i)).start()
        if to is None:
            rows_in[pl.ds(sp, 1)] = rows_out[pl.ds(sp, 1)]
        else:
            remote(rows_out.at[sp], rows_in.at[sp], rows_send, rows_recv, (to, sp)).start()

    def rows_sent(count=SP - 1):
        return remote(rows_out.at[pl.ds(0, count)], rows_in.at[pl.ds(0, count)], rows_send, rows_recv, partner)

    def collect_rows(ref, count=SP - 1):
        rows_sent(count).wait_recv()
        gather = (ci == (ri % R) // 4 * 16 + ri // R * 4 + ri % 4).astype(BF)
        own = dot_nn(gather, rows_in[...].reshape(256, 256))
        for k in range(4):
            ref[R:2 * R, 256 * k:256 * (k + 1)] = own[R * k:R * (k + 1)].astype(ref.dtype)

    def shift(n, k, ref, recv, device):
        return remote(state.at[n], ref.at[n], shift_send.at[k], recv.at[n], (device, sp))

    def shifted(k):
        return remote(state, arrived, shift_send.at[k], shift_recv.at[0], partner)

    def arrive(n):
        remote(state.at[n], arrived.at[n], shift_send.at[0], shift_recv.at[n], partner).wait_recv()

    def u_arrive(n):
        remote(u_out.at[n], u_in.at[n], u_send.at[0], u_recv.at[n], partner).wait_recv()

    u_sent = remote(u_out, u_in, u_send.at[0], u_recv.at[0], (5, sp))
    d_sent = remote(dbuf.at[0], d_in, u_send.at[1], d_recv, (4, sp))

    give_u = remote(u_in, u_in, u_send.at[0], u_recv.at[0], partner)
    give_v = remote(d_in, d_in, u_send.at[1], d_recv, partner)
    when(is_a & (y == 1), core_q.start)
    when(gives_d & (tm != 7), core_d.start)

    @pl.when(gives_c)
    def _():
        for turn in range(4):
            core_part(turn).start()

    @pl.when(is_a)
    def _():
        when(y != 3, core_d.wait_recv)

        @pl.when(y == 3)
        def _():
            def columns(n):
                remote(u_out.at[n], u_in.at[n], u_send.at[0], u_recv.at[n], (5, sp)).start()
            loop(4, columns)
            d_sent.start()

        @pl.when(y == 2)
        def _():
            total = None
            for n in range(4):
                u_arrive(n)
                term = dot_nn(u_in[n], wt[1, block(n), :])
                total = term if total is None else total + term
            set_x(x2, total.astype(BF))
            turns = iter(range(4))

            def chunk(q):
                core_part(next(turns)).wait_recv()
                return product_chunk(0)(q)
            exchange(1, packed(chunk), 7, True)
        @pl.when(y != 2)
        def _():
            set_x(x2, dbuf[1])
            set_x(x3, dbuf[0])
            exchange(0, paired(level_chunk))
        send_positions()
        when(y == 2, lambda: transpose_w(0, 0))
        when(y == 3, lambda: send_rows(dbuf[1], 7))

        when(y < 2, core_c_here)

        @pl.when(y != 2)
        def _():
            collect(0, True)
            e = (dot_nn(zbuf[0:R], wt[0]) + zbuf[R:2 * R].astype(F32)).astype(BF)
            for n in range(4):
                state[n] = e[:, 256 * n:256 * (n + 1)]

            @pl.when(y == 3)
            def _():
                for n in range(4):
                    shift(n, 0, arrived, shift_recv, 4).start()

            @pl.when(y == 1)
            def _():
                for n in range(4):
                    shift(n, 0, u_in, u_recv, 1).start()

        @pl.when(y == 2)
        def _():
            collect(0, True, SP)
            vterm[...] = zbuf[...].astype(F32)
            collect(2, False, SP, True)
            total = vterm[0:R]
            for n in range(4):
                arrive(n)
                t = (arrived[n].astype(F32) + zbuf[0:R, block(n)].astype(F32)).astype(BF)
                total = total + dot_nn(t, wt[1, block(n), :])
            x2[R:2 * R] = total.astype(BF)

            def third(n):
                state[n] = (dot_nn(x2[R:2 * R], wt[0, :, block(n)]) + vterm[R:2 * R, block(n)]).astype(BF)
                shift(n, 0, arrived, shift_recv, 1).start()
            loop(4, third)
            for k, device in ((1, 2), (2, 3)):
                for n in range(4):
                    shift(n, k, arrived, shift_recv, device).start()
        make_perm()
        set_x_blocks(state)
        exchange(3, packed(transpose_chunk, perm_chunk))

        @pl.when(y < 2)
        def _():
            def rows(q):
                w[2, block(q), :] = dot_nn(w[0, block(q), :], w[1]).astype(BF)
            loop(4, rows)
            transpose_w(1, 2)
            make_wp(2)
        collect(3)

        @pl.when(y < 2)
        def _():
            eterm[...] = zbuf[...].astype(F32)

        @pl.when(y == 2)
        def _():
            sent_final[...] = zbuf[...]

        @pl.when(y == 3)
        def _():
            final[...] = zbuf[...]

    @pl.when(is_b & (y < 3))
    def _():
        @pl.when(y == 2)
        def _():
            core_d.wait_recv()
            set_x(x2, dbuf[1])
            set_x(x3, dbuf[0])
            exchange(0, paired(level_chunk), 5)
        send_positions()
        send_rows(dbuf[1])

        @pl.when(y == 1)
        def _():
            core_q.wait_recv()
            w[2, block(quarter), :] = dot_nn(w[0, block(quarter), :], w[1]).astype(BF)
            for k in range(4):
                part(2, k).start()
        eterm[0:R] = dbuf[1].astype(F32)

        @pl.when(y == 2)
        def _():
            core_c_here()
            transpose_w(1, 1)
            d_sent.wait_recv()
            set_x(x2, dot_nn(d_in[...], wt[1]).astype(BF))
            exchange(1, packed(product_chunk(0)), 5, True, 2)
        make_perm()
        for k in range(4):
            when(y == 0, lambda: share(k))
            wp[block(k), :] = dot_nn(perm[block(k), :], w[1]).astype(BF)
        collect_rows(eterm)

    @pl.when(is_b & (y == 3))
    def _():
        core_c_here()
        transpose_w(0, 0)
        final[0:R] = dbuf[1]
        collect_rows(final, SP)
        collect(1, False, SP, True)
        for n in range(4):
            state[n] = dot_nn(zbuf[0:R], wt[0, :, block(n)]).astype(BF)
            shift(n, 0, arrived, shift_recv, 5).start()

    slot = jnp.where(is_a, 2, 1)
    ends = (y < 2) | (is_b & (y == 2))

    @pl.when(y == 0)
    def _():
        @pl.when(is_b)
        def _():
            loop(4, u_arrive)
            give_u.start()

        @pl.when(is_a)
        def _():
            give_u.wait_recv()
        set_x_blocks(u_in)
        exchange(1, packed(product_chunk(slot), wp_chunk))

        @pl.when(is_b)
        def _():
            shared.wait_recv()
            copy_core.start()
            transpose_w(2, 3)

    @pl.when(ends)
    def _():
        @pl.when((y == 0) & is_b)
        def _():
            total = None
            for n in range(4):
                arrive(n)
                term = dot_nn(arrived[n], wt[2, block(n), :])
                total = term if total is None else total + term
            d_in[...] = total.astype(BF)
            give_v.start()
            set_x(x2, d_in[...])

        @pl.when((y == 0) & is_a)
        def _():
            give_v.wait_recv()
            set_x(x2, d_in[...])

        @pl.when(y > 0)
        def _():
            loop(4, arrive)
            set_x_blocks(arrived)
        exchange(2, packed(product_chunk(slot), wp_chunk))

        @pl.when(y == 0)
        def _():
            @pl.when(is_a)
            def _():
                copy_core.wait_recv()
                transpose_w(2, 3)
            loop(4, lambda k: wt.__setitem__((0, block(k)), dot_nn(wt[2, block(k), :], wt[1]).astype(BF)))
            collect(1)
            eterm[...] = eterm[...] + dot_nn(zbuf[...], wt[1])
        collect(2)

        @pl.when(y == 0)
        def _():
            final[...] = (eterm[...] + dot_nn(zbuf[...], wt[0])).astype(BF)

        @pl.when(y > 0)
        def _():
            out = (eterm[...] + dot_nn(zbuf[...], wt[1])).astype(BF)
            when(y == 1, lambda: final.__setitem__(Ellipsis, out))
            when(y == 2, lambda: sent_final.__setitem__(Ellipsis, out))

    @pl.when(y == 2)
    def _():
        swap = remote(sent_final, final, swap_send, swap_recv, partner)
        swap.start()
        swap.wait()

    sigma_ref[...] = final[0:R]
    load_b.wait()
    column = lax.broadcasted_iota(jnp.int32, (1, N), 1) // 128
    chosen = jnp.zeros((1, N), jnp.int32)
    for n in range(pattern_ref.shape[1]):
        chosen = jnp.where(column == pattern[0, n], 1, chosen)
    masked = jnp.where(chosen == 1, final[R:2 * R].astype(F32), 0.0).astype(BF)
    grad_ref[...] = dot_nn(masked, basis[...]).astype(BF)

    when(gives_d, core_d.wait_send)
    when(gives_c, core_c.wait_send)
    when((y == 0) & is_b, copy_core.wait_send)
    when(is_b & (y < 3), rows_sent().wait_send)
    when(is_a & (y == 3), rows_sent(SP).wait_send)
    when(is_a | (y < 3), positions.wait_send)
    when(is_a & (y != 2), exchanged(0).wait_send)
    when(is_b & (y == 2), exchanged(0, SP).wait_send)
    when(is_b & (y == 2), exchanged(1, SP, True).wait_send)
    when(y == 0, exchanged(1).wait_send)
    when(is_a & (y == 2), exchanged(1, SP, True).wait_send)
    when(ends, exchanged(2).wait_send)
    when(is_a, exchanged(3).wait_send)
    when((is_a & (y > 0)) | (is_b & (y == 3)), shifted(0).wait_send)
    when(is_a & (y == 2), shifted(1).wait_send)
    when(is_a & (y == 2), shifted(2).wait_send)
    when(is_b & (y == 0), give_v.wait_send)
    when(is_b & (y == 0), give_u.wait_send)
    when(is_a & (y == 3), u_sent.wait_send)
    when(is_a & (y == 3), d_sent.wait_send)
    when(is_b & (y == 1), parts_sent(0).wait_send)
    when(is_a & (y == 1), core_q.wait_send)
    when(is_b & (y == 0), shared.wait_send)


def on_device(dinv, coupling, owner_position, pattern, basis):
    vmem = pl.BlockSpec(memory_space=pltpu.VMEM)
    hbm = pl.BlockSpec(memory_space=pltpu.HBM)
    h = basis.shape[1]
    dma = pltpu.SemaphoreType.DMA
    operands = (dinv[0], coupling[0], owner_position[None], pattern, basis)
    sigma, gradient = pl.pallas_call(
        kernel,
        out_shape=(jax.ShapeDtypeStruct((R, N), BF), jax.ShapeDtypeStruct((R, h), BF)),
        in_specs=[hbm] * len(operands),
        out_specs=(vmem, vmem),
        scratch_shapes=[
            pltpu.VMEM((4, N, N), BF),
            pltpu.VMEM((3, N, N), BF),
            pltpu.VMEM((N, N), BF),
            pltpu.VMEM((N, N), BF),
            pltpu.VMEM((2 * R, N), BF),
            pltpu.VMEM((2 * R, N), BF),
            pltpu.VMEM((2 * R, N), BF),
            pltpu.VMEM((2, R, N), BF),
            pltpu.VMEM((2 * R, N), F32),
            pltpu.VMEM((2 * R, N), F32),
            pltpu.VMEM((4, R, 256), BF),
            pltpu.VMEM((4, R, 256), BF),
            pltpu.VMEM((4, R, 256), BF),
            pltpu.VMEM((4, R, 256), BF),
            pltpu.VMEM((R, N), BF),
            pltpu.VMEM((2 * R, N), BF),
            pltpu.VMEM((2 * R, N), BF),
            pltpu.VMEM((N, h), BF),
            pltpu.VMEM((1, R), jnp.int32),
            pltpu.VMEM((8, 128), jnp.int32),
            pltpu.VMEM((SP, 8, 128), jnp.int32),
            pltpu.SMEM((1, 4), jnp.int32),
            pltpu.VMEM((4, SP, 2, 32, 128), BF),
            pltpu.VMEM((4, SP, 2, 32, 128), BF),
            pltpu.VMEM((SP, 16, 256), BF),
            pltpu.VMEM((SP, 16, 256), BF),
            dma((5,)), dma((3,)), dma((3,)), dma((4,)), dma((4,)), dma((2,)), dma((4,)), dma, dma((4,)), dma((4,)),
            dma, dma, dma, dma, dma, dma, dma, dma((4,)), dma, dma, dma((4,)),
        ],
        compiler_params=pltpu.CompilerParams(
            collective_id=0, has_side_effects=True, vmem_limit_bytes=48 << 20),
        name="selected_inverse",
    )(*[pltpu.with_memory_space_constraint(a, pltpu.HBM) for a in operands])
    return sigma[None], gradient[None]


def solution(mesh):
    placed = (P("tm", "space", None), P("tm", None, None), P("space"), P("space", None), P())
    return jax.shard_map(
        on_device,
        mesh=mesh,
        in_specs=placed,
        out_specs=(P("tm", "space", None), P("tm", "space", None)),
        check_vma=False,
    )
```

```python
import jax
import jax.numpy as jnp
from jax import lax
from jax.experimental import pallas as pl
from jax.experimental.pallas import tpu as pltpu
from jax.sharding import PartitionSpec as P

MESH = pl.DeviceIdType.MESH
N = 1024
R = 64
SP = 16
F32 = jnp.float32
BF = jnp.bfloat16
FAR_FIRST = (10, 6, 14, 2, 9, 11, 5, 7, 13, 15, 1, 3, 8, 4, 12)

ONE_TO_ONE = ((1, 0), (2, 0), (2, 1), (2, 3), (3, 1), (3, 2), (5, 1), (5, 2), (5, 3), (5, 4), (6, 4), (6, 5), (7, 5), (7, 6))
ALL_TO_ALL = tuple((t, t) for t in range(7)) + ((4, 5), (5, 7), (6, 7))


def dot_nt(a, b):
    return lax.dot_general(a, b, (((1,), (1,)), ((), ())), preferred_element_type=F32)


def dot_nn(a, b):
    return jnp.dot(a, b, preferred_element_type=F32)


def kernel(
    dinv_ref, coupling_ref, pos_ref, pattern_ref, basis_ref,
    sigma_ref, grad_ref,
    w, wt, wp, perm, x2, x3, zbuf, dbuf, eterm, vterm, state, arrived, u_out, u_in, d_in, sent_final, final, basis,
    pos, pos_out, pos_in, pattern, pieces_out, pieces_in, rows_out, rows_in,
    local_sem, core_send, core_recv, shift_send, shift_recv, u_send, u_recv, d_recv, ex_send, ex_recv,
    rows_send, rows_recv, swap_send, swap_recv, pos_send, pos_recv, part_send, part_recv, share_send, share_recv, part_in,
):
    tm, sp = lax.axis_index("tm"), lax.axis_index("space")
    y, c = tm // 2, tm % 2
    zc, xc = sp // 4, sp % 4
    partner = (y * 2 + 1 - c, sp)
    is_a = c == jnp.where(y == 2, 1, 0)
    is_b = jnp.logical_not(is_a)
    quarter = (zc % 2) * 2 + xc % 2

    def when(condition, work):
        pl.when(condition)(work)

    def loop(count, work):
        for index in range(count):
            work(index)

    def block(index, size=256):
        if isinstance(index, int):
            return slice(size * index, size * (index + 1))
        return pl.ds(pl.multiple_of(size * index, size), size)

    def remote(src, dst, send, recv, device):
        return pltpu.make_async_remote_copy(
            src_ref=src, dst_ref=dst, send_sem=send, recv_sem=recv, device_id=device, device_id_type=MESH)

    load_d = pltpu.make_async_copy(dinv_ref, dbuf.at[c], local_sem.at[0])
    load_c = pltpu.make_async_copy(coupling_ref, w.at[c], local_sem.at[1])
    load_p = pltpu.make_async_copy(pos_ref, pos, local_sem.at[2])
    load_t = pltpu.make_async_copy(pattern_ref, pattern, local_sem.at[3])
    load_b = pltpu.make_async_copy(basis_ref, basis, local_sem.at[4])
    for load in (load_d, load_c, load_p, load_t, load_b):
        load.start()

    barrier = pltpu.get_barrier_semaphore()

    def greet(t, s):
        pl.semaphore_signal(barrier, inc=1, device_id=(t, s), device_id_type=MESH)

    for t in range(8):
        @pl.when(tm == t)
        def _():
            for source, to in ALL_TO_ALL:
                if to == t:
                    for d in FAR_FIRST + ((0,) if source != to else ()):
                        greet(source, (sp + d) % SP)
            for source, to in ONE_TO_ONE:
                if to == t:
                    greet(source, sp)
    greets = sum(jnp.where(tm == t, sum(SP - (a == b) for a, b in ALL_TO_ALL if a == t) + sum(a == t for a, _ in ONE_TO_ONE), 0)
                 for t in range(8))

    lane = lax.broadcasted_iota(jnp.int32, (1, 1, 128), 2)
    low = lane < R
    lo = low[0]
    pick = low != (sp % 2 == 1)
    pick2 = pick[0]
    ri = lax.broadcasted_iota(jnp.int32, (256, 256), 0)
    ci = lax.broadcasted_iota(jnp.int32, (256, 256), 1)
    eye = (ri == ci).astype(BF)

    def transpose_w(to, slot):
        loop(4, lambda p: wt.__setitem__((to, slice(None), block(p)), w[slot, block(p), :].T))

    core_d = remote(dbuf.at[c], dbuf.at[c], core_send.at[0], core_recv.at[0], partner)
    load_d.wait()

    @pl.when(tm == 7)
    def _():
        pl.semaphore_wait(barrier, greets)
        core_d.start()
    load_c.wait()
    when((c == 0) & (y != 2), lambda: transpose_w(0, 0))
    when((c == 1) & (y < 3), lambda: transpose_w(1, 1))
    load_p.wait()
    load_t.wait()

    @pl.when(tm == 6)
    def _():
        core_d.wait_recv()
        for n in range(4):
            u_out[n] = dot_nn(dbuf[1], wt[0, :, block(n)]).astype(BF)

    @pl.when(tm != 7)
    def _():
        pl.semaphore_wait(barrier, greets)

    core_c = remote(w.at[c], w.at[c], core_send.at[1], core_recv.at[1], partner)

    def core_part(turn):
        rows = block((zc + (2, 1, 3, 0)[turn]) % 4)
        return remote(w.at[c, rows], w.at[c, rows], core_send.at[1], part_in.at[turn], partner)

    def core_c_here():
        for turn in range(4):
            core_part(turn).wait_recv()

    copy_core = remote(w.at[3], w.at[3], core_send.at[2], core_recv.at[2], partner)

    def copy_rows(rows):
        return remote(w.at[3, rows], w.at[3, rows], core_send.at[2], core_recv.at[2], partner)

    core_q = remote(w.at[0, block(quarter)], w.at[0, block(quarter)], core_send.at[2], core_recv.at[2], partner)
    gives_d = (c == 1) | (y == 2)
    gives_c = ((c == 1) & (y < 3)) | ((c == 0) & (y > 1))

    def part(slot, k):
        rows = pl.ds(pl.multiple_of(256 * quarter + 64 * k, 64), 64)
        return remote(w.at[slot, rows], w.at[3, rows], part_send, part_recv.at[k], (((y + 3) % 4) * 2 + 1, sp))

    def parts_sent(slot):
        return remote(w.at[slot, pl.ds(0, 256)], w.at[3, pl.ds(0, 256)], part_send, part_recv.at[0], partner)

    def share(k):
        part(3, k).wait_recv()
        first = 256 * quarter + 64 * k
        copy_rows(pl.ds(pl.multiple_of(first, 64), 64)).start()
        xs, zs = ((xc + 1) % 4, (xc + 3) % 4), ((zc + 1) % 4, (zc + 3) % 4)
        to = [(4 * zs[0] + xs[0], 0, 16), (4 * zs[0] + xs[1], 16, 16), (4 * zs[1] + xs[0], 32, 16), (4 * zs[1] + xs[1], 48, 16),
              (4 * zc + xs[0], 0, 32), (4 * zc + xs[1], 32, 32), (4 * zs[0] + xc, 0, 32), (4 * zs[1] + xc, 32, 32)]
        for device, offset, count in to:
            rows = pl.ds(pl.multiple_of(first + offset, 16), count)
            remote(w.at[3, rows], w.at[3, rows], share_send, share_recv, (tm, device)).start()

    shared = remote(w.at[3, pl.ds(0, 768)], w.at[3, pl.ds(0, 768)], share_send, share_recv, partner)

    def set_x(ref, value):
        ref[0:R] = value
        ref[R:2 * R] = value

    def set_x_blocks(blocks):
        for n in range(4):
            for h in range(2):
                x2[R * h:R * (h + 1), 256 * n:256 * (n + 1)] = blocks[n]

    def piece(ref, k, i, single):
        return ref.at[k, i, 0] if single else ref.at[k, i]

    def exchange(k, make, to=None, single=False, into=None):
        for dz in (2, 1, 3, 0):
            q = (zc + dz) % 4
            make(q, pieces_out.at[k, pl.ds(4 * q, 4)])
            for dx in (2, 1, 3, 0):
                i = 4 * q + (xc + dx) % 4
                if dz or dx or to is not None:
                    slot = k if into is None else into
                    remote(piece(pieces_out, k, i, single), piece(pieces_in, slot, sp, single), ex_send.at[k], ex_recv.at[slot],
                           (tm if to is None else to, i)).start()
        if to is None:
            pieces_in[k, pl.ds(sp, 1)] = pieces_out[k, pl.ds(sp, 1)]

    def exchanged(k, count=SP - 1, single=False):
        some = pl.ds(0, count)
        return remote(piece(pieces_out, k, some, single), piece(pieces_in, k, some, single), ex_send.at[k], ex_recv.at[k], partner)

    def packed(*chunks):
        def make(q, out):
            for h, chunk in enumerate(chunks):
                v = chunk(q).reshape(4, 2, 32, 128)
                out[:, h] = jnp.where(pick, v[:, 0], v[:, 1]).astype(BF)
        return make

    def paired(chunk):
        def make(q, out):
            out[...] = chunk(q).reshape(4, 2, 32, 128).astype(BF)
        return make

    def collect(k, pair=False, count=SP - 1, single=False):
        exchanged(k, count, single).wait_recv()

        def columns(m):
            for h in range(1 if single else 2):
                a = pieces_in[k, 2 * m, h].astype(F32)
                b = pieces_in[k, 2 * m + 1, h].astype(F32)
                one, two = (32 * h, R + 32 * h) if pair else (R * h, R * h + 32)
                zbuf[one:one + 32, block(m, 128)] = jnp.where(lo, a, b).astype(BF)
                zbuf[two:two + 32, block(m, 128)] = pltpu.roll(jnp.where(lo, b, a), R, 1).astype(BF)
        loop(8, columns)

    def product_chunk(slot):
        return lambda q: dot_nt(w[slot, block(q), :], x2[...])

    def transpose_chunk(q):
        return dot_nt(eye, x2[:, block(q)])

    def perm_chunk(q):
        return dot_nt(perm[block(q), :], x2[...])

    def wp_chunk(q):
        return dot_nt(wp[block(q), :], x2[...])

    def level_chunk(q):
        return jnp.where(pick2, dot_nt(w[0, block(q), :], x2[...]), dot_nt(eye, x3[:, block(q)]))

    def send_positions():
        pos_out[...] = jnp.broadcast_to(jnp.concatenate([pos[...], pos[...]], axis=1), (8, 128))
        for d in FAR_FIRST:
            remote(pos_out, pos_in.at[sp], pos_send, pos_recv, (tm, (sp + d) % SP)).start()
        pos_in[pl.ds(sp, 1)] = pos_out[...][None]

    positions = remote(pos_in.at[pl.ds(0, SP - 1)], pos_in.at[pl.ds(0, SP - 1)], pos_send, pos_recv, partner)

    def make_perm():
        positions.wait_recv()
        p_index = lax.broadcasted_iota(jnp.int32, (N, 128), 0)

        def columns(m):
            row = jnp.where(lo, pos_in[2 * m, 0:1], pos_in[2 * m + 1, 0:1])
            perm[:, block(m, 128)] = (p_index == row).astype(BF)
        loop(8, columns)

    def make_wp(slot):
        loop(4, lambda p: wp.__setitem__((block(p), slice(None)), dot_nn(perm[block(p), :], w[slot]).astype(BF)))

    def send_rows(value, to=None):
        position = pos[...]
        target = position // R * 4 + position % 4
        place = (lax.broadcasted_iota(jnp.int32, (R, R), 0) == target).astype(BF)
        ordered = dot_nn(place, value).astype(BF)
        stacked = jnp.concatenate([ordered[:, 256 * k:256 * (k + 1)] for k in range(4)], axis=0)
        spread = (ci == (ri % 16) // 4 * R + ri // 16 * 4 + ri % 4).astype(BF)
        rows_out[...] = dot_nn(spread, stacked).astype(BF).reshape(SP, 16, 256)
        for d in FAR_FIRST:
            i = (sp + d) % SP
            remote(rows_out.at[i], rows_in.at[sp], rows_send, rows_recv, (tm if to is None else to, i)).start()
        if to is None:
            rows_in[pl.ds(sp, 1)] = rows_out[pl.ds(sp, 1)]
        else:
            remote(rows_out.at[sp], rows_in.at[sp], rows_send, rows_recv, (to, sp)).start()

    def rows_sent(count=SP - 1):
        return remote(rows_out.at[pl.ds(0, count)], rows_in.at[pl.ds(0, count)], rows_send, rows_recv, partner)

    def collect_rows(ref, count=SP - 1):
        rows_sent(count).wait_recv()
        gather = (ci == (ri % R) // 4 * 16 + ri // R * 4 + ri % 4).astype(BF)
        own = dot_nn(gather, rows_in[...].reshape(256, 256))
        for k in range(4):
            ref[R:2 * R, 256 * k:256 * (k + 1)] = own[R * k:R * (k + 1)].astype(ref.dtype)

    def shift(n, k, ref, recv, device):
        return remote(state.at[n], ref.at[n], shift_send.at[k], recv.at[n], (device, sp))

    def shifted(k):
        return remote(state, arrived, shift_send.at[k], shift_recv.at[0], partner)

    def arrive(n):
        remote(state.at[n], arrived.at[n], shift_send.at[0], shift_recv.at[n], partner).wait_recv()

    def u_arrive(n):
        remote(u_out.at[n], u_in.at[n], u_send.at[0], u_recv.at[n], partner).wait_recv()

    u_sent = remote(u_out, u_in, u_send.at[0], u_recv.at[0], (5, sp))
    d_sent = remote(dbuf.at[0], d_in, u_send.at[1], d_recv, (4, sp))

    give_v = remote(d_in, d_in, u_send.at[1], d_recv, partner)
    when(is_a & (y == 1), core_q.start)
    when(gives_d & (tm != 7), core_d.start)

    @pl.when(gives_c)
    def _():
        for turn in range(4):
            core_part(turn).start()

    @pl.when(is_a)
    def _():
        when(y != 3, core_d.wait_recv)

        @pl.when(y == 3)
        def _():
            def columns(n):
                remote(u_out.at[n], u_in.at[n], u_send.at[0], u_recv.at[n], (5, sp)).start()
            loop(4, columns)
            d_sent.start()

        @pl.when(y == 2)
        def _():
            total = None
            for n in range(4):
                u_arrive(n)
                term = dot_nn(u_in[n], wt[1, block(n), :])
                total = term if total is None else total + term
            set_x(x2, total.astype(BF))
            turns = iter(range(4))

            def chunk(q):
                core_part(next(turns)).wait_recv()
                return product_chunk(0)(q)
            exchange(1, packed(chunk), 7, True)
        @pl.when(y != 2)
        def _():
            set_x(x2, dbuf[1])
            set_x(x3, dbuf[0])
            exchange(0, paired(level_chunk))
        send_positions()
        when(y == 2, lambda: transpose_w(0, 0))
        when(y == 3, lambda: send_rows(dbuf[1], 7))

        when(y < 2, core_c_here)

        @pl.when(y != 2)
        def _():
            collect(0, True)
            e = (dot_nn(zbuf[0:R], wt[0]) + zbuf[R:2 * R].astype(F32)).astype(BF)
            for n in range(4):
                state[n] = e[:, 256 * n:256 * (n + 1)]

            @pl.when(y == 3)
            def _():
                for n in range(4):
                    shift(n, 0, arrived, shift_recv, 4).start()

            @pl.when(y == 1)
            def _():
                for core in (0, 1):
                    for n in range(4):
                        shift(n, core, u_in, u_recv, core).start()

        @pl.when(y == 2)
        def _():
            collect(0, True, SP)
            vterm[...] = zbuf[...].astype(F32)
            collect(2, False, SP, True)
            total = vterm[0:R]
            for n in range(4):
                arrive(n)
                t = (arrived[n].astype(F32) + zbuf[0:R, block(n)].astype(F32)).astype(BF)
                total = total + dot_nn(t, wt[1, block(n), :])
            x2[R:2 * R] = total.astype(BF)

            def third(n):
                state[n] = (dot_nn(x2[R:2 * R], wt[0, :, block(n)]) + vterm[R:2 * R, block(n)]).astype(BF)
                shift(n, 0, arrived, shift_recv, 1).start()
            loop(4, third)
            for k, device in ((1, 2), (2, 3)):
                for n in range(4):
                    shift(n, k, arrived, shift_recv, device).start()
        make_perm()
        set_x_blocks(state)
        exchange(3, packed(transpose_chunk, perm_chunk))

        @pl.when(y < 2)
        def _():
            def rows(q):
                w[2, block(q), :] = dot_nn(w[0, block(q), :], w[1]).astype(BF)
            loop(4, rows)
            transpose_w(1, 2)
            make_wp(2)
        @pl.when(y > 1)
        def _():
            collect(3)
            when(y == 2, lambda: sent_final.__setitem__(Ellipsis, zbuf[...]))
            when(y == 3, lambda: final.__setitem__(Ellipsis, zbuf[...]))

    @pl.when(is_b & (y < 3))
    def _():
        @pl.when(y == 2)
        def _():
            core_d.wait_recv()
            set_x(x2, dbuf[1])
            set_x(x3, dbuf[0])
            exchange(0, paired(level_chunk), 5)
        send_positions()
        send_rows(dbuf[1])

        @pl.when(y == 1)
        def _():
            core_q.wait_recv()
            w[2, block(quarter), :] = dot_nn(w[0, block(quarter), :], w[1]).astype(BF)
            for k in range(4):
                part(2, k).start()
        eterm[0:R] = dbuf[1].astype(F32)

        @pl.when(y == 2)
        def _():
            core_c_here()
            transpose_w(1, 1)
            d_sent.wait_recv()
            set_x(x2, dot_nn(d_in[...], wt[1]).astype(BF))
            exchange(1, packed(product_chunk(0)), 5, True, 2)
        make_perm()
        for k in range(4):
            when(y == 0, lambda: share(k))
            wp[block(k), :] = dot_nn(perm[block(k), :], w[1]).astype(BF)
        collect_rows(eterm)

    @pl.when(is_b & (y == 3))
    def _():
        core_c_here()
        transpose_w(0, 0)
        final[0:R] = dbuf[1]
        collect_rows(final, SP)
        collect(1, False, SP, True)
        for n in range(4):
            state[n] = dot_nn(zbuf[0:R], wt[0, :, block(n)]).astype(BF)
            shift(n, 0, arrived, shift_recv, 5).start()

    slot = jnp.where(is_a, 2, 1)
    ends = (y < 2) | (is_b & (y == 2))

    @pl.when(y == 0)
    def _():
        loop(4, u_arrive)
        set_x_blocks(u_in)
        exchange(1, packed(product_chunk(slot), wp_chunk))

        @pl.when(is_b)
        def _():
            shared.wait_recv()
            for d in (1, 2, 3):
                copy_rows(block((quarter + d) % 4)).start()
            transpose_w(2, 3)

    @pl.when(ends)
    def _():
        @pl.when((y == 0) & is_b)
        def _():
            total = None
            for n in range(4):
                arrive(n)
                term = dot_nn(arrived[n], wt[2, block(n), :])
                total = term if total is None else total + term
            d_in[...] = total.astype(BF)
            give_v.start()
            set_x(x2, d_in[...])

        @pl.when((y == 0) & is_a)
        def _():
            give_v.wait_recv()
            set_x(x2, d_in[...])

        @pl.when(y > 0)
        def _():
            loop(4, arrive)
            set_x_blocks(arrived)
        exchange(2, packed(product_chunk(slot), wp_chunk))

        @pl.when(is_a)
        def _():
            collect(3)
            eterm[...] = zbuf[...].astype(F32)

        @pl.when(y == 0)
        def _():
            @pl.when(is_a)
            def _():
                copy_core.wait_recv()
                transpose_w(2, 3)
            loop(4, lambda k: wt.__setitem__((0, block(k)), dot_nn(wt[2, block(k), :], wt[1]).astype(BF)))
            collect(1)
            eterm[...] = eterm[...] + dot_nn(zbuf[...], wt[1])
        collect(2)

        @pl.when(y == 0)
        def _():
            final[...] = (eterm[...] + dot_nn(zbuf[...], wt[0])).astype(BF)

        @pl.when(y > 0)
        def _():
            out = (eterm[...] + dot_nn(zbuf[...], wt[1])).astype(BF)
            when(y == 1, lambda: final.__setitem__(Ellipsis, out))
            when(y == 2, lambda: sent_final.__setitem__(Ellipsis, out))

    @pl.when(y == 2)
    def _():
        swap = remote(sent_final, final, swap_send, swap_recv, partner)
        swap.start()
        swap.wait()

    sigma_ref[...] = final[0:R]
    load_b.wait()
    column = lax.broadcasted_iota(jnp.int32, (1, N), 1) // 128
    chosen = jnp.zeros((1, N), jnp.int32)
    for n in range(pattern_ref.shape[1]):
        chosen = jnp.where(column == pattern[0, n], 1, chosen)
    masked = jnp.where(chosen == 1, final[R:2 * R].astype(F32), 0.0).astype(BF)
    grad_ref[...] = dot_nn(masked, basis[...]).astype(BF)

    when(gives_d, core_d.wait_send)
    when(gives_c, core_c.wait_send)
    when((y == 0) & is_b, copy_core.wait_send)
    when(is_b & (y < 3), rows_sent().wait_send)
    when(is_a & (y == 3), rows_sent(SP).wait_send)
    when(is_a | (y < 3), positions.wait_send)
    when(is_a & (y != 2), exchanged(0).wait_send)
    when(is_b & (y == 2), exchanged(0, SP).wait_send)
    when(is_b & (y == 2), exchanged(1, SP, True).wait_send)
    when(y == 0, exchanged(1).wait_send)
    when(is_a & (y == 2), exchanged(1, SP, True).wait_send)
    when(ends, exchanged(2).wait_send)
    when(is_a, exchanged(3).wait_send)
    when((is_a & (y > 0)) | (is_b & (y == 3)), shifted(0).wait_send)
    when(is_a & ((y == 1) | (y == 2)), shifted(1).wait_send)
    when(is_a & (y == 2), shifted(2).wait_send)
    when(is_b & (y == 0), give_v.wait_send)
    when(is_a & (y == 3), u_sent.wait_send)
    when(is_a & (y == 3), d_sent.wait_send)
    when(is_b & (y == 1), parts_sent(0).wait_send)
    when(is_a & (y == 1), core_q.wait_send)
    when(is_b & (y == 0), shared.wait_send)


def on_device(dinv, coupling, owner_position, pattern, basis):
    vmem = pl.BlockSpec(memory_space=pltpu.VMEM)
    hbm = pl.BlockSpec(memory_space=pltpu.HBM)
    h = basis.shape[1]
    dma = pltpu.SemaphoreType.DMA
    operands = (dinv[0], coupling[0], owner_position[None], pattern, basis)
    sigma, gradient = pl.pallas_call(
        kernel,
        out_shape=(jax.ShapeDtypeStruct((R, N), BF), jax.ShapeDtypeStruct((R, h), BF)),
        in_specs=[hbm] * len(operands),
        out_specs=(vmem, vmem),
        scratch_shapes=[
            pltpu.VMEM((4, N, N), BF),
            pltpu.VMEM((3, N, N), BF),
            pltpu.VMEM((N, N), BF),
            pltpu.VMEM((N, N), BF),
            pltpu.VMEM((2 * R, N), BF),
            pltpu.VMEM((2 * R, N), BF),
            pltpu.VMEM((2 * R, N), BF),
            pltpu.VMEM((2, R, N), BF),
            pltpu.VMEM((2 * R, N), F32),
            pltpu.VMEM((2 * R, N), F32),
            pltpu.VMEM((4, R, 256), BF),
            pltpu.VMEM((4, R, 256), BF),
            pltpu.VMEM((4, R, 256), BF),
            pltpu.VMEM((4, R, 256), BF),
            pltpu.VMEM((R, N), BF),
            pltpu.VMEM((2 * R, N), BF),
            pltpu.VMEM((2 * R, N), BF),
            pltpu.VMEM((N, h), BF),
            pltpu.VMEM((1, R), jnp.int32),
            pltpu.VMEM((8, 128), jnp.int32),
            pltpu.VMEM((SP, 8, 128), jnp.int32),
            pltpu.SMEM((1, 4), jnp.int32),
            pltpu.VMEM((4, SP, 2, 32, 128), BF),
            pltpu.VMEM((4, SP, 2, 32, 128), BF),
            pltpu.VMEM((SP, 16, 256), BF),
            pltpu.VMEM((SP, 16, 256), BF),
            dma((5,)), dma((3,)), dma((3,)), dma((4,)), dma((4,)), dma((2,)), dma((4,)), dma, dma((4,)), dma((4,)),
            dma, dma, dma, dma, dma, dma, dma, dma((4,)), dma, dma, dma((4,)),
        ],
        compiler_params=pltpu.CompilerParams(
            collective_id=0, has_side_effects=True, vmem_limit_bytes=48 << 20),
        name="selected_inverse",
    )(*[pltpu.with_memory_space_constraint(a, pltpu.HBM) for a in operands])
    return sigma[None], gradient[None]


def solution(mesh):
    placed = (P("tm", "space", None), P("tm", None, None), P("space"), P("space", None), P())
    return jax.shard_map(
        on_device,
        mesh=mesh,
        in_specs=placed,
        out_specs=(P("tm", "space", None), P("tm", "space", None)),
        check_vma=False,
    )
```
